1024 devices in a mesh: dp: 8 (over y), ctx: 16 (over z_hi, x, core), tp: 8 (over z_lo).
Axes of the slice: x: 4, y: 8, z: 16 (z_hi: 2, z_lo: 8; z = z_hi * 8 + z_lo), core: 2. Of those that a mesh axis runs over, the one named last changes fastest.
Arguments:
- tokens: bfloat16 [16384, 6144], P(('dp', 'ctx')), may hold values from -6 to 6
- router_weight: bfloat16 [6144, 16], replicated, may hold values from -0.15625 to 0.15625
- expert_hidden: bfloat16 [8, 56, 16, 16, 5376], P('dp', None, 'ctx', None, 'tp'), may hold values from -6 to 6
- down_weight: bfloat16 [16, 5376, 3072], P('ctx', 'tp'), may hold values from -0.109375 to 0.109375
- expert_ids: int32 [16384, 4], P(('dp', 'ctx')), may hold values from 0 to 15, as said below
- mixed_grad: bfloat16 [16384, 3072], P(('dp', 'ctx')), may hold values from -6 to 6
Outputs:
- combined: bfloat16 [16384, 3072], P(('dp', 'ctx'), 'tp')
- row_grads: bfloat16 [8, 56, 16, 16, 3072], P('dp', None, 'ctx', None, 'tp')
- router_grad: float32 [6144, 16], replicated
The draws below stay inside these ranges and needn't reach their ends.
Inputs may be any that keep to these rules, and one draw needn't show every extreme that they name: `expert_ids`: each token names 4 different experts. Among the 128 tokens of one index of dp and ctx no expert is named by more than 56 tokens, and one expert, the same for all such groups, is named by exactly 56 of them in every group.
All inputs are finite; a program needn't handle non-finite values.
Results may differ from the reference program's by a relative error of at most 0.02.
Values may be sent and summed in bfloat16 or wider, within the bound.
A program may use at most 64 MiB of HBM per device.

```python
import jax
import jax.numpy as jnp
from jax import lax

DM = 6144
EXPERTS = 16
TOPK = 4
FF = 5376
DW = 3072
TOK_DEV = 128
CAP = 56
REPLICAS = 8
SOURCES = 16
BLOCKS = 8
TOKENS = 16384


def draw_expert_ids(key, part):
    key = jax.random.fold_in(key, 7)
    groups = TOKENS // TOK_DEV
    hot_expert = jax.random.randint(jax.random.fold_in(key, 1), (), 0, EXPERTS)
    group_keys = jax.random.split(jax.random.fold_in(key, 2), groups)
    length = EXPERTS + TOPK
    token_rank = jnp.arange(TOK_DEV, dtype=jnp.int32)
    lane_index = jnp.arange(TOPK, dtype=jnp.int32)

    def one_group(group_key):
        key_order = jax.random.fold_in(group_key, 1)
        key_others = jax.random.fold_in(group_key, 2)
        key_first = jax.random.fold_in(group_key, 3)
        key_second = jax.random.fold_in(group_key, 4)
        key_shuffle = jax.random.fold_in(group_key, 5)
        token_order = jax.random.permutation(key_order, TOK_DEV)
        others = jax.random.permutation(key_others, EXPERTS - 1).astype(jnp.int32)
        others = others + (others >= hot_expert).astype(jnp.int32)
        cycle_list = jnp.concatenate([others, others[:TOPK + 1]])
        start_one = jax.random.randint(key_first, (), 0, EXPERTS - 1)
        start_two = jax.random.randint(key_second, (), 0, length)
        first_index = (start_one + (TOPK - 1) * token_rank[:, None] + lane_index[None, :TOPK - 1]) % (EXPERTS - 1)
        first_picks = others[first_index]
        hot_rows = jnp.concatenate([jnp.full((TOK_DEV, 1), hot_expert, jnp.int32), first_picks], axis=1)
        cold_index = (start_two + TOPK * (token_rank[:, None] - CAP) + lane_index[None, :]) % length
        cold_rows = cycle_list[cold_index]
        picks_all = jnp.where(token_rank[:, None] < CAP, hot_rows, cold_rows)
        scores = jax.random.randint(key_shuffle, (TOK_DEV, TOPK), 0, 1 << 20) * TOPK + lane_index[None, :]
        shuffle = jnp.argsort(scores, axis=1)
        picks_all = jnp.take_along_axis(picks_all, shuffle, axis=1)
        return jnp.zeros((TOK_DEV, TOPK), jnp.int32).at[token_order].set(picks_all)
    return jax.vmap(one_group)(group_keys).reshape(TOKENS, TOPK)


def with_spikes(entries, own_key, source, target, shards_of, factor):
    def block_of(position):
        return (jnp.arange(entries.shape[position]) // (entries.shape[position] // shards_of)).reshape((-1,) + (1,) * (entries.ndim - 1 - position))

    first = jax.random.permutation(own_key, shards_of)[block_of(target)]
    other_side = (block_of(target) + shards_of // 2) % shards_of
    return jnp.where((block_of(source) == first) | (block_of(source) == other_side), factor * entries, entries)


def steps_of(own_key, dims, cuts, low, top_value):
    def one(position, blocks):
        draws = jax.random.uniform(jax.random.fold_in(jax.random.fold_in(own_key, 6), position), (blocks,), jnp.float32, low / len(cuts), top_value / len(cuts))
        return jnp.repeat(jnp.exp(draws), dims[position] // blocks).reshape((-1,) + (1,) * (len(dims) - position - 1))

    factor_of = one(*cuts[0])
    for cut in cuts[1:]:
        factor_of = factor_of * one(*cut)
    return factor_of


def scatter_about(stream_key, extent, scale, limit, cuts=(), kind=jnp.bfloat16):
    loudness = steps_of(stream_key, extent, cuts, -0.22, 0.18) if cuts else 1.0
    array = jax.random.normal(stream_key, extent, jnp.float32) * scale * loudness
    return jnp.minimum(jnp.maximum(array, -limit), limit).astype(kind)


def noise_with(stream_key, extent, deviation, reach, cuts, heavy, kind=jnp.bfloat16):
    drawn = deviation * jax.random.normal(stream_key, extent, jnp.float32)
    if cuts:
        drawn = drawn * steps_of(stream_key, extent, cuts, -0.22, 0.18)
    return jnp.clip(with_spikes(drawn, jax.random.fold_in(stream_key, 3), *heavy), -reach, reach).astype(kind)


def setup_inputs(seed: int = 0) -> dict:
    keys = jax.random.split(jax.random.key(seed), 7)
    return {
        "tokens": scatter_about(keys[0], (TOKENS, DM), 1.0, 6.0, ((0, 128),)),
        "router_weight": scatter_about(keys[1], (DM, EXPERTS), (DM // 4) ** -0.5, 0.15625),
        "expert_hidden": scatter_about(keys[2], (REPLICAS, CAP, EXPERTS, SOURCES, FF), 1.0, 6.0, ((0, 8), (2, 16), (4, 8))),
        "down_weight": noise_with(keys[3], (EXPERTS, FF, DW), FF ** -0.5, 0.109375, ((0, 16), (1, 8)), (1, 2, 8, 2.0)),
        "expert_ids": draw_expert_ids(jax.random.fold_in(keys[6], 71), 0),
        "mixed_grad": scatter_about(keys[5], (TOKENS, DW), 1.0, 6.0, ((0, 128),)),
    }


def group_slots(expert_ids):
    onehot = (expert_ids[..., None] == jnp.arange(EXPERTS, dtype=jnp.int32)).astype(jnp.int32)
    flat_hits = onehot.reshape(expert_ids.shape[0], -1, EXPERTS)
    before = jnp.cumsum(flat_hits, axis=1) - flat_hits
    return jnp.sum(before * flat_hits, axis=2).reshape(expert_ids.shape)


def reference(tokens, router_weight, expert_hidden, down_weight, expert_ids, mixed_grad):
    groups = REPLICAS * SOURCES
    logits = jnp.dot(tokens, router_weight, preferred_element_type=jnp.float32)
    onehot = expert_ids[:, :, None] == jnp.arange(EXPERTS, dtype=jnp.int32)[None, None, :]
    chosen = jnp.sum(jnp.where(onehot, logits[:, None, :], 0.0), axis=2)
    weights = jnp.exp(chosen)
    gate_values = weights / jnp.sum(weights, axis=1, keepdims=True)
    slot_index = group_slots(expert_ids.reshape(groups, TOK_DEV, TOPK)).reshape(TOKENS, TOPK)
    block_width = FF // BLOCKS
    source_index = jnp.arange(SOURCES, dtype=jnp.int32)

    def replica_rows(operands):
        hidden, slots_here, ids_here = operands
        running_sum = jnp.zeros((CAP, EXPERTS, SOURCES, DW), jnp.float32)
        for block_index in range(BLOCKS):
            low_edge = block_index * block_width
            block_part = jnp.einsum(
                "cesf,efd->cesd",
                hidden[..., low_edge:low_edge + block_width].astype(jnp.float32),
                down_weight[:, low_edge:low_edge + block_width, :].astype(jnp.float32),
            )
            rounded = lax.optimization_barrier(block_part.astype(jnp.bfloat16))
            running_sum = running_sum + rounded.astype(jnp.float32)
        expert_out = running_sum.astype(jnp.bfloat16)
        return expert_out[slots_here, ids_here, source_index[:, None, None]]

    picked = lax.map(
        replica_rows,
        (
            expert_hidden,
            slot_index.reshape(REPLICAS, SOURCES, TOK_DEV, TOPK),
            expert_ids.reshape(REPLICAS, SOURCES, TOK_DEV, TOPK),
        ),
    )
    picked = picked.reshape(TOKENS, TOPK, DW).astype(jnp.float32)
    combined = jnp.einsum("tk,tkd->td", gate_values, picked).astype(jnp.bfloat16)
    gate_grad = jnp.einsum("tkd,td->tk", picked, mixed_grad.astype(jnp.float32))
    mix_term = jnp.sum(gate_values * gate_grad, axis=1, keepdims=True)
    chosen_grad = gate_values * (gate_grad - mix_term)
    logit_grad = jnp.sum(jnp.where(onehot, chosen_grad[:, :, None], 0.0), axis=1)
    router_grad = jnp.dot(tokens.astype(jnp.float32).T, logit_grad, precision=lax.Precision.HIGHEST) / TOK_DEV
    grad_values = (gate_values[:, :, None] * mixed_grad[:, None, :].astype(jnp.float32)).astype(jnp.bfloat16)
    token_group = jnp.arange(TOKENS, dtype=jnp.int32) // TOK_DEV
    replica = (token_group // SOURCES)[:, None]
    source = (token_group % SOURCES)[:, None]
    row_grads = jnp.zeros((REPLICAS, CAP, EXPERTS, SOURCES, DW), jnp.bfloat16)
    row_grads = row_grads.at[replica, slot_index, expert_ids, source].set(grad_values)
    return combined, row_grads, router_grad
```

```python
import jax
import jax.numpy as jnp
from jax import lax
from jax.experimental import pallas as pl
from jax.experimental.pallas import tpu as pltpu
from jax.sharding import PartitionSpec as P

MESH = pl.DeviceIdType.MESH


def router_kernel(
    gg_ref, gate_ref, tok_ref, out_ref,
    gg_all, tok_cols, part, from_dp, from_ctx, tok_sem,
    send0, recv0, send1, recv1, send2, recv2, send3, recv3, send4, recv4,
):
    dp, ctx, tp = lax.axis_index("dp"), lax.axis_index("ctx"), lax.axis_index("tp")
    n_dp, n_ctx, n_tp = lax.axis_size("dp"), lax.axis_size("ctx"), lax.axis_size("tp")
    width = tok_cols.shape[1]
    columns = pl.ds(pl.multiple_of(tp * width, 128), width)
    load = pltpu.make_async_copy(tok_ref.at[:, columns], tok_cols, tok_sem)
    load.start()

    def at_dp(k):
        return (lax.rem(dp + k, n_dp), ctx, tp)

    def at_ctx(k):
        return (dp, lax.rem(ctx + k, n_ctx), tp)

    def at_tp(k):
        return (dp, ctx, lax.rem(tp + k, n_tp))

    barrier = pltpu.get_barrier_semaphore()
    for count, where in ((n_tp, at_tp), (n_dp, at_dp), (n_ctx, at_ctx)):
        @pl.loop(1, count)
        def _(k):
            pl.semaphore_signal(barrier, inc=1, device_id=where(k), device_id_type=MESH)
    pl.semaphore_wait(barrier, n_tp + n_dp + n_ctx - 3)

    def exchange(count, me, where, source, target, send, recv):
        def copy(k, slot):
            return pltpu.make_async_remote_copy(
                src_ref=source(lax.rem(me + k, count)),
                dst_ref=target(slot),
                send_sem=send.at[lax.rem(me + k, count)],
                recv_sem=recv.at[slot],
                device_id=where(k),
                device_id_type=MESH,
            )

        @pl.loop(1, count)
        def _(k):
            copy(k, me).start()

        @pl.loop(1, count)
        def _(k):
            copy(k, lax.rem(me + k, count)).wait_recv()

        @pl.loop(1, count)
        def _(k):
            copy(k, me).wait_send()

    gg_all[tp] = gg_ref[...]
    exchange(n_tp, tp, at_tp, lambda k: gg_ref, lambda k: gg_all.at[k], send0, recv0)
    gate_grad = gg_all[0]
    for k in range(1, n_tp):
        gate_grad = gate_grad + gg_all[k]
    gates = gate_ref[...]
    mix_term = jnp.sum(gates * gate_grad, axis=0, keepdims=True)
    logit_grad = gates * (gate_grad - mix_term)
    high = logit_grad.astype(jnp.bfloat16)
    rest = logit_grad - high.astype(jnp.float32)
    middle = rest.astype(jnp.bfloat16)
    low = (rest - middle.astype(jnp.float32)).astype(jnp.bfloat16)
    load.wait()
    token_cols = tok_cols[...]
    product = jnp.dot(low, token_cols, preferred_element_type=jnp.float32)
    product += jnp.dot(middle, token_cols, preferred_element_type=jnp.float32)
    product += jnp.dot(high, token_cols, preferred_element_type=jnp.float32)
    product = product * (1.0 / tok_cols.shape[0])
    experts = product.shape[0]
    each, lanes = experts // n_dp, width // 128
    for e in range(experts):
        for k in range(lanes):
            row = (e % each) * lanes + k
            part[e // each, row // 4, row % 4 : row % 4 + 1, :] = product[e : e + 1, k * 128 : (k + 1) * 128]

    from_dp[dp] = part[dp]
    exchange(n_dp, dp, at_dp, lambda k: part.at[k], lambda k: from_dp.at[k], send1, recv1)
    total = from_dp[0]
    for k in range(1, n_dp):
        total = total + from_dp[k]
    from_ctx[ctx] = total
    exchange(n_ctx, ctx, at_ctx, lambda k: from_ctx.at[ctx], lambda k: from_ctx.at[k], send2, recv2)
    total = from_ctx[0]
    for k in range(1, n_ctx):
        total = total + from_ctx[k]
    out_ref[dp, tp] = total
    exchange(n_tp, tp, at_tp, lambda k: out_ref.at[dp, tp], lambda k: out_ref.at[dp, k], send3, recv3)
    exchange(n_dp, dp, at_dp, lambda k: out_ref.at[dp], lambda k: out_ref.at[k], send4, recv4)


def router_sum(gate_part, gates, tokens):
    n_dp, n_ctx, n_tp = lax.axis_size("dp"), lax.axis_size("ctx"), lax.axis_size("tp")
    experts, tok_count = gates.shape
    width = tokens.shape[1] // n_tp
    each, lanes = experts // n_dp, width // 128
    chunk = (each * lanes // 4, 4, 128)
    vmem = pl.BlockSpec(memory_space=pltpu.VMEM)
    sems = [pltpu.SemaphoreType.DMA((n,)) for n in (n_tp, n_tp, n_dp, n_dp, n_ctx, n_ctx, n_tp, n_tp, n_dp, n_dp)]
    gathered = pl.pallas_call(
        router_kernel,
        out_shape=jax.ShapeDtypeStruct((n_dp, n_tp) + chunk, jnp.float32),
        in_specs=[vmem, vmem, pl.BlockSpec(memory_space=pl.ANY)],
        out_specs=vmem,
        scratch_shapes=[
            pltpu.VMEM((n_tp, experts, tok_count), jnp.float32),
            pltpu.VMEM((tok_count, width), jnp.bfloat16),
            pltpu.VMEM((n_dp,) + chunk, jnp.float32),
            pltpu.VMEM((n_dp,) + chunk, jnp.float32),
            pltpu.VMEM((n_ctx,) + chunk, jnp.float32),
            pltpu.SemaphoreType.DMA,
        ] + sems,
        compiler_params=pltpu.CompilerParams(collective_id=1, has_side_effects=True, vmem_limit_bytes=16 << 20),
        name="router_sum",
    )(gate_part, gates, tokens)
    gathered = gathered.reshape(n_dp, n_tp, each, lanes, 128)
    return gathered.transpose(1, 3, 4, 0, 2).reshape(tokens.shape[1], experts)


def per_device(tokens, router_weight, expert_hidden, down_weight, expert_ids, mixed_grad):
    tp_ranks = lax.axis_size("tp")
    tp_index = lax.axis_index("tp")
    hidden = expert_hidden[0]
    capacity = hidden.shape[0]
    experts_all = router_weight.shape[1]
    full_width = mixed_grad.shape[1]
    col_width = full_width // tp_ranks
    tok_count = tokens.shape[0]
    top_count = expert_ids.shape[1]
    logits = jnp.dot(tokens, router_weight, preferred_element_type=jnp.float32)
    onehot = expert_ids[:, :, None] == jnp.arange(experts_all, dtype=jnp.int32)[None, None, :]
    chosen = jnp.sum(jnp.where(onehot, logits[:, None, :], 0.0), axis=2)
    weights = jnp.exp(chosen)
    gate_values = weights / jnp.sum(weights, axis=1, keepdims=True)
    flat_hits = onehot.reshape(tok_count * top_count, experts_all).astype(jnp.int32)
    before = jnp.cumsum(flat_hits, axis=0) - flat_hits
    slot_index = jnp.sum(before * flat_hits, axis=1).reshape(tok_count, top_count)
    route_index = (slot_index * experts_all + expert_ids).reshape(-1)
    grad_cols = lax.dynamic_slice_in_dim(mixed_grad, tp_index * col_width, col_width, 1)
    partial_sum = jnp.einsum(
        "fd,rf->dr", down_weight[0], hidden.reshape(-1, hidden.shape[-1]), preferred_element_type=jnp.float32
    ).astype(jnp.bfloat16)
    summed = lax.psum_scatter(partial_sum, "tp", scatter_dimension=0, tiled=True)
    summed = summed.T.reshape(capacity, 1, experts_all, col_width)
    arrived = lax.all_to_all(summed, "ctx", split_axis=2, concat_axis=1, tiled=True)
    row_table = arrived.reshape(capacity * experts_all, col_width)
    picked = (
        jnp.take(row_table, route_index, axis=0)
        .reshape(tok_count, top_count, col_width)
        .astype(jnp.float32)
    )
    combined = jnp.einsum("tk,tkd->td", gate_values, picked).astype(jnp.bfloat16)
    gate_part = jnp.einsum("tkd,td->tk", picked, grad_cols.astype(jnp.float32))
    gate_map = jnp.sum(jnp.where(onehot, gate_values[:, :, None], 0.0), axis=1).T
    part_map = jnp.sum(jnp.where(onehot, gate_part[:, :, None], 0.0), axis=1).T
    router_grad = router_sum(part_map, gate_map, tokens)
    grad_values = (gate_values[:, :, None] * grad_cols[:, None, :].astype(jnp.float32)).astype(
        jnp.bfloat16
    )
    buffer = jnp.zeros((capacity * experts_all, col_width), jnp.bfloat16)
    buffer = buffer.at[route_index].set(grad_values.reshape(-1, col_width))
    outgoing = buffer.reshape(capacity, experts_all, 1, col_width)
    incoming = lax.all_to_all(outgoing, "ctx", split_axis=1, concat_axis=2, tiled=True)
    row_grads = incoming[None]
    return (combined, row_grads, router_grad)


def solution(mesh):
    return jax.shard_map(
        per_device,
        mesh=mesh,
        in_specs=(
            P(("dp", "ctx"), None),
            P(),
            P("dp", None, "ctx", None, "tp"),
            P("ctx", "tp", None),
            P(("dp", "ctx"), None),
            P(("dp", "ctx"), None),
        ),
        out_specs=(P(("dp", "ctx"), "tp"), P("dp", None, "ctx", None, "tp"), P()),
        check_vma=False,
    )
```

```python
import jax
import jax.numpy as jnp
from jax import lax
from jax.experimental import pallas as pl
from jax.experimental.pallas import tpu as pltpu
from jax.sharding import PartitionSpec as P

MESH = pl.DeviceIdType.MESH
AHEAD = 3


def layer_kernel(
    rows_ref, weight_ref, grad_ref, info_ref, gate_ref, tok_ref,
    comb_ref, slot_grad_ref, router_ref,
    weight, grads, tok_cols, made, arrived, passed_in, passed_out, mix, chosen, dots, total,
    info, gg_out, gg_all, comb_out, comb_in, grad_out, part, from_dp, from_ctx,
    load_sem, tok_sem, weight_sem, x_send, x_recv, z_send, z_recv, mg_send, mg_recv,
    pair_send, pair_recv, rg_send, rg_recv, gg_send, gg_recv,
    send1, recv1, send2, recv2, send3, recv3, send4, recv4,
):
    dp, ctx, z = lax.axis_index("dp"), lax.axis_index("ctx"), lax.axis_index("tp")
    n_dp, n_ctx, n_z = lax.axis_size("dp"), lax.axis_size("ctx"), lax.axis_size("tp")
    n_q = n_ctx // 2
    half, q = ctx // n_q, lax.rem(ctx, n_q)
    last = n_z - 1
    cols = grads.shape[2]
    toks = grad_ref.shape[0]
    own_rows = pl.ds(pl.multiple_of(half * toks, toks), toks)
    other_rows = pl.ds(pl.multiple_of((1 - half) * toks, toks), toks)

    def at_dp(k):
        return (lax.rem(dp + k, n_dp), ctx, z)

    def at_ctx(k):
        return (dp, lax.rem(ctx + k, n_ctx), z)

    def at_z(k):
        return (dp, ctx, lax.rem(z + k, n_z))

    def at_q(k):
        return (dp, half * n_q + lax.rem(q + k, n_q), z)

    def remote(src, dst, send, recv, device):
        return pltpu.make_async_remote_copy(
            src_ref=src, dst_ref=dst, send_sem=send, recv_sem=recv, device_id=device, device_id_type=MESH
        )

    pair = (dp, (1 - half) * n_q + q, z)
    upper = (dp, ctx, jnp.minimum(z + 1, last))
    lower = (dp, ctx, jnp.maximum(z - 1, 0))

    flip = z // (n_z // 2)
    near = z + flip * (last - 2 * z)

    def block_at(n):
        later = n - (last - 2 * near)
        reach = near - later // 2
        inner = near + reach - 2 * reach * lax.rem(later + 2 * n_z, 2)
        block = jnp.where(later < 0, last - n, inner)
        return block + flip * (last - 2 * block)

    width = tok_cols.shape[1]
    tok_load = pltpu.make_async_copy(
        tok_ref.at[:, pl.ds(pl.multiple_of(z * width, 128), width)], tok_cols, tok_sem
    )
    tok_load.start()

    def weight_load(b):
        return pltpu.make_async_copy(
            weight_ref.at[:, pl.ds(pl.multiple_of(b * cols, 128), cols)], weight.at[b], weight_sem.at[b]
        )

    def grad_load(b):
        return pltpu.make_async_copy(
            grad_ref.at[:, pl.ds(pl.multiple_of(b * cols, 128), cols)], grads.at[b, own_rows], load_sem.at[b]
        )

    @pl.loop(0, n_z)
    def _(n):
        weight_load(block_at(n)).start()

    @pl.loop(0, n_z)
    def _(b):
        grad_load(b).start()

    barrier = pltpu.get_barrier_semaphore()
    for count, where in ((n_z, at_z), (n_dp, at_dp), (n_ctx, at_ctx)):
        @pl.loop(1, count)
        def _(k):
            pl.semaphore_signal(barrier, inc=1, device_id=where(k), device_id_type=MESH)

    @pl.loop(1, n_z)
    def _(k):
        there = (dp, (1 - half) * n_q + q, lax.rem(z + k, n_z))
        pl.semaphore_signal(barrier, inc=1, device_id=there, device_id_type=MESH)

    @pl.loop(0, n_z)
    def _(b):
        grad_load(b).wait()

    pl.semaphore_wait(barrier, 2 * n_z + n_dp + n_ctx - 4)

    info[half] = info_ref[half]
    pair_info = remote(info_ref.at[1 - half], info.at[half], pair_send.at[0], pair_recv.at[0], pair)
    pair_grad = remote(grads.at[z, own_rows], grads.at[z, own_rows], pair_send.at[1], pair_recv.at[1], pair)
    got_info = remote(info_ref.at[half], info.at[1 - half], pair_send.at[0], pair_recv.at[0], pair)
    got_grad = remote(grads.at[z, other_rows], grads.at[z, other_rows], pair_send.at[1], pair_recv.at[1], pair)
    pair_info.start()
    pair_grad.start()

    def x_copy(b, k):
        to = lax.rem(q + k, n_q)
        return remote(made.at[b, to], arrived.at[b, q], x_send.at[b, to], x_recv.at[b, q], at_q(k))

    def x_wait(b, k):
        come = lax.rem(q + k, n_q)
        return remote(made.at[b, come], arrived.at[b, come], x_send.at[b, come], x_recv.at[b, come], at_q(k))

    def produce(n):
        b = block_at(n)
        weight_load(b).wait()

        @pl.loop(0, n_q // 2)
        def _(r):
            rows = rows_ref[pl.ds(2 * r, 2)]
            size = rows.shape[1]
            product = jnp.dot(
                rows.reshape(2 * size, rows.shape[2]), weight[b], preferred_element_type=jnp.float32
            )
            made[b, pl.ds(2 * r, 2)] = product.astype(jnp.bfloat16).reshape(2, size, cols)

        @pl.loop(1, n_q)
        def _(k):
            x_copy(b, k).start()

        arrived[b, q] = made[b, q]

    for n in range(AHEAD):
        produce(n)

    got_info.wait_recv()
    per_q = rows_ref.shape[1]
    experts_here = n_q

    def chosen_mask():
        code = jnp.concatenate([info[0, 1], info[1, 1]], axis=1)
        spot = lax.broadcasted_iota(jnp.int32, (experts_here, per_q, 2 * toks), 1).astype(jnp.float32)
        return jnp.broadcast_to(code[:, None, :], spot.shape) == spot

    mask = chosen_mask()
    gate = jnp.concatenate([info[0, 0], info[1, 0]], axis=1)
    spread = jnp.where(mask, jnp.broadcast_to(gate[:, None, :], mask.shape), 0.0)
    spread = spread.reshape(experts_here * per_q, 2 * toks)
    chosen[...] = jnp.where(mask, 1.0, 0.0).reshape(spread.shape).astype(jnp.bfloat16)
    turned = spread.T
    high = turned.astype(jnp.bfloat16)
    mix[0] = high
    mix[1] = (turned - high.astype(jnp.float32)).astype(jnp.bfloat16)
    row_gate = jnp.sum(spread, axis=1, keepdims=True)
    dots[...] = jnp.zeros(dots.shape, jnp.float32)

    got_grad.wait_recv()
    picked_grad = jnp.dot(chosen[...], grads[z], preferred_element_type=jnp.float32) * row_gate
    grad_out[...] = picked_grad.astype(jnp.bfloat16).reshape(grad_out.shape)
    slot_grad_ref[q] = grad_out[q]

    def rg_copy(k):
        to = lax.rem(q + k, n_q)
        return remote(grad_out.at[to], slot_grad_ref.at[q], rg_send.at[to], rg_recv.at[q], at_q(k))

    def rg_wait(k):
        come = lax.rem(q + k, n_q)
        return remote(grad_out.at[come], slot_grad_ref.at[come], rg_send.at[come], rg_recv.at[come], at_q(k))

    @pl.loop(1, n_q)
    def _(k):
        rg_copy(k).start()

    def mg_copy(b, device):
        here = grads.at[b, other_rows]
        return remote(here, here, mg_send.at[b], mg_recv.at[b], device)

    def mg_copy_low(b, device):
        here = grads.at[b, other_rows]
        return remote(here, here, mg_send.at[n_z + b], mg_recv.at[b], device)

    def mg_step(j):
        below, above = z - j, z + j

        @pl.when((j > 0) & (below >= 0))
        def _():
            mg_copy(below, lower).wait_recv()

        @pl.when((j > 0) & (above <= last))
        def _():
            mg_copy(above, upper).wait_recv()

        @pl.when((below >= 0) & (z < last))
        def _():
            mg_copy(below, upper).start()

        @pl.when((above <= last) & (z > 0))
        def _():
            mg_copy_low(above, lower).start()

    def mg_finish(j):
        below, above = z - j, z + j

        @pl.when((below >= 0) & (z < last))
        def _():
            mg_copy(below, upper).wait_send()

        @pl.when((above <= last) & (z > 0))
        def _():
            mg_copy_low(above, lower).wait_send()

    def mixed(b):
        rows = arrived[b].reshape(n_q * per_q, cols)
        return jnp.dot(mix[0], rows, preferred_element_type=jnp.float32) + jnp.dot(
            mix[1], rows, preferred_element_type=jnp.float32
        )

    def add_dots(b):
        rows = arrived[b].reshape(n_q * per_q, cols)
        dots[...] += lax.dot_general(
            rows, grads[b], (((1,), (1,)), ((), ())), preferred_element_type=jnp.float32
        )

    def z_copy(b, slot, device):
        return remote(passed_out.at[b], passed_in.at[slot], z_send.at[b], z_recv.at[slot], device)

    def x_wait_all(b):
        @pl.loop(1, n_q)
        def _(k):
            x_wait(b, k).wait_recv()

    @pl.loop(0, last)
    def _(n):
        b = block_at(n)
        x_wait_all(b)

        @pl.when(n + AHEAD < n_z)
        def _():
            produce(n + AHEAD)

        @pl.when(n < n_z // 2)
        def _():
            mg_step(2 * n)
            mg_step(2 * n + 1)

        total[...] = mixed(b)
        up = b > z

        @pl.when((up & (z > 0)) | (jnp.logical_not(up) & (z < last)))
        def _():
            z_copy(b, b, lower).wait_recv()
            total[...] += passed_in[b].astype(jnp.float32)

        passed_out[b] = total[...].astype(jnp.bfloat16)

        @pl.when(up)
        def _():
            z_copy(b, b, upper).start()

        @pl.when(b < z - 1)
        def _():
            z_copy(b, b, lower).start()

        @pl.when(b == z - 1)
        def _():
            z_copy(b, n_z, lower).start()

        @pl.when(n == n_z // 2)
        def _():
            @pl.loop(0, n_z // 2)
            def _(m):
                add_dots(block_at(m))

        @pl.when(n >= n_z // 2)
        def _():
            add_dots(b)

    x_wait_all(z)
    add_dots(z)
    gate_grad = jnp.where(chosen_mask(), dots[...].reshape(experts_here, per_q, 2 * toks), 0.0)
    gate_grad = jnp.sum(gate_grad, axis=1)
    gg_out[0] = gate_grad[:, :toks]
    gg_out[1] = gate_grad[:, toks:]
    gg_all[half * n_z + z] = gg_out[half]
    spot = half * n_z + z

    def gg_copy(k, slot):
        to = lax.rem(spot + k, 2 * n_z)
        to_half = to // n_z
        return remote(
            gg_out.at[to_half], gg_all.at[slot], gg_send.at[to], gg_recv.at[slot],
            (dp, to_half * n_q + q, lax.rem(to, n_z)),
        )

    @pl.loop(1, 2 * n_z)
    def _(k):
        gg_copy(k, spot).start()

    total[...] = mixed(z)

    @pl.when(z > 0)
    def _():
        z_copy(z, z, lower).wait_recv()
        total[...] += passed_in[z].astype(jnp.float32)

    @pl.when(z < last)
    def _():
        z_copy(z, n_z, upper).wait_recv()
        total[...] += passed_in[n_z].astype(jnp.float32)

    comb_out[...] = total[other_rows, :].astype(jnp.bfloat16)
    pair_comb = remote(comb_out, comb_in, pair_send.at[2], pair_recv.at[2], pair)
    pair_comb.start()

    @pl.loop(1, 2 * n_z)
    def _(k):
        gg_copy(k, lax.rem(spot + k, 2 * n_z)).wait_recv()

    parts = []
    for h in range(2):
        summed = gg_all[h * n_z]
        for k in range(1, n_z):
            summed = summed + gg_all[h * n_z + k]
        parts.append(summed)
    gate_grad = jnp.concatenate(parts, axis=0)
    gates = gate_ref[...]
    mix_term = jnp.sum(gates * gate_grad, axis=0, keepdims=True)
    logit_grad = gates * (gate_grad - mix_term)
    high = logit_grad.astype(jnp.bfloat16)
    rest = logit_grad - high.astype(jnp.float32)
    middle = rest.astype(jnp.bfloat16)
    low = (rest - middle.astype(jnp.float32)).astype(jnp.bfloat16)
    tok_load.wait()
    token_cols = tok_cols[...]
    product = jnp.dot(low, token_cols, preferred_element_type=jnp.float32)
    product += jnp.dot(middle, token_cols, preferred_element_type=jnp.float32)
    product += jnp.dot(high, token_cols, preferred_element_type=jnp.float32)
    product = product * (1.0 / toks)
    experts = product.shape[0]
    each, lanes = experts // n_dp, width // 128
    for e in range(experts):
        for k in range(lanes):
            row = (e % each) * lanes + k
            part[e // each, row // 4, row % 4 : row % 4 + 1, :] = product[e : e + 1, k * 128 : (k + 1) * 128]

    def exchange(count, me, where, source, target, send, recv):
        def copy(k, slot):
            to = lax.rem(me + k, count)
            return remote(source(to), target(slot), send.at[to], recv.at[slot], where(k))

        @pl.loop(1, count)
        def _(k):
            copy(k, me).start()

        @pl.loop(1, count)
        def _(k):
            copy(k, lax.rem(me + k, count)).wait_recv()

        @pl.loop(1, count)
        def _(k):
            copy(k, me).wait_send()

    from_dp[dp] = part[dp]
    exchange(n_dp, dp, at_dp, lambda k: part.at[k], lambda k: from_dp.at[k], send1, recv1)
    summed = from_dp[0]
    for k in range(1, n_dp):
        summed = summed + from_dp[k]
    from_ctx[ctx] = summed
    exchange(n_ctx, ctx, at_ctx, lambda k: from_ctx.at[ctx], lambda k: from_ctx.at[k], send2, recv2)
    summed = from_ctx[0]
    for k in range(1, n_ctx):
        summed = summed + from_ctx[k]
    router_ref[dp, z] = summed
    exchange(n_z, z, at_z, lambda k: router_ref.at[dp, z], lambda k: router_ref.at[dp, k], send3, recv3)
    exchange(n_dp, dp, at_dp, lambda k: router_ref.at[dp], lambda k: router_ref.at[k], send4, recv4)

    remote(comb_out, comb_in, pair_send.at[2], pair_recv.at[2], pair).wait_recv()
    comb_ref[...] = (total[own_rows, :] + comb_in[...].astype(jnp.float32)).astype(jnp.bfloat16)

    @pl.loop(1, n_q)
    def _(k):
        rg_wait(k).wait_recv()

    pair_info.wait_send()
    pair_grad.wait_send()
    pair_comb.wait_send()

    @pl.loop(1, n_q)
    def _(k):
        rg_copy(k).wait_send()

    @pl.loop(1, 2 * n_z)
    def _(k):
        gg_copy(k, spot).wait_send()

    @pl.loop(0, n_z)
    def _(j):
        mg_finish(j)

        @pl.loop(1, n_q)
        def _(k):
            x_copy(j, k).wait_send()

        @pl.when(j != z)
        def _():
            z_copy(j, j, lower).wait_send()


def layer(rows, weight, grad, info, gates, tokens):
    n_dp, n_ctx, n_z = lax.axis_size("dp"), lax.axis_size("ctx"), lax.axis_size("tp")
    n_q = n_ctx // 2
    per_q, depth = rows.shape[1:]
    full = weight.shape[1]
    cols = full // n_z
    experts, toks = gates.shape
    width = tokens.shape[1] // n_z
    each, lanes = experts // n_dp, width // 128
    chunk = (each * lanes // 4, 4, 128)
    vmem = pl.BlockSpec(memory_space=pltpu.VMEM)
    anywhere = pl.BlockSpec(memory_space=pl.ANY)
    bf16, f32 = jnp.bfloat16, jnp.float32
    dma = pltpu.SemaphoreType.DMA
    scratch = [
        pltpu.VMEM((n_z, depth, cols), bf16),
        pltpu.VMEM((n_z, 2 * toks, cols), bf16),
        pltpu.VMEM((toks, width), bf16),
        pltpu.VMEM((n_z, n_q, per_q, cols), bf16),
        pltpu.VMEM((n_z, n_q, per_q, cols), bf16),
        pltpu.VMEM((n_z + 1, 2 * toks, cols), bf16),
        pltpu.VMEM((n_z, 2 * toks, cols), bf16),
        pltpu.VMEM((2, 2 * toks, n_q * per_q), bf16),
        pltpu.VMEM((n_q * per_q, 2 * toks), bf16),
        pltpu.VMEM((n_q * per_q, 2 * toks), f32),
        pltpu.VMEM((2 * toks, cols), f32),
        pltpu.VMEM((2, 2, n_q, toks), f32),
        pltpu.VMEM((2, n_q, toks), f32),
        pltpu.VMEM((2 * n_z, n_q, toks), f32),
        pltpu.VMEM((toks, cols), bf16),
        pltpu.VMEM((toks, cols), bf16),
        pltpu.VMEM((n_q, per_q, cols), bf16),
        pltpu.VMEM((n_dp,) + chunk, f32),
        pltpu.VMEM((n_dp,) + chunk, f32),
        pltpu.VMEM((n_ctx,) + chunk, f32),
        dma((n_z,)), dma, dma((n_z,)),
        dma((n_z, n_q)), dma((n_z, n_q)),
        dma((n_z,)), dma((n_z + 1,)),
        dma((2 * n_z,)), dma((n_z,)),
        dma((3,)), dma((3,)),
        dma((n_q,)), dma((n_q,)),
        dma((2 * n_z,)), dma((2 * n_z,)),
        dma((n_dp,)), dma((n_dp,)), dma((n_ctx,)), dma((n_ctx,)),
        dma((n_z,)), dma((n_z,)), dma((n_dp,)), dma((n_dp,)),
    ]
    return pl.pallas_call(
        layer_kernel,
        out_shape=(
            jax.ShapeDtypeStruct((toks, cols), bf16),
            jax.ShapeDtypeStruct((n_q, per_q, cols), bf16),
            jax.ShapeDtypeStruct((n_dp, n_z) + chunk, f32),
        ),
        in_specs=[vmem, anywhere, anywhere, vmem, vmem, anywhere],
        out_specs=(vmem, vmem, vmem),
        scratch_shapes=scratch,
        compiler_params=pltpu.CompilerParams(collective_id=1, has_side_effects=True, vmem_limit_bytes=56 << 20),
        name="layer",
    )(rows, weight, grad, info, gates, tokens)


def per_device(tokens, router_weight, expert_hidden, down_weight, expert_ids, mixed_grad):
    ctx_ranks, tp_ranks, dp_ranks = lax.axis_size("ctx"), lax.axis_size("tp"), lax.axis_size("dp")
    half = lax.axis_index("ctx") // (ctx_ranks // 2)
    hidden = expert_hidden[0, :, 0]
    capacity, sources, depth = hidden.shape
    experts = router_weight.shape[1]
    tok_count = tokens.shape[0]
    group = sources // 2
    rows = hidden.reshape(capacity, 2, group, depth).transpose(2, 1, 0, 3)
    rows = rows.reshape(group, 2 * capacity, depth)

    logits = lax.dot_general(
        router_weight, tokens, (((0,), (1,)), ((), ())), preferred_element_type=jnp.float32
    )
    names = jnp.arange(experts, dtype=jnp.int32)[:, None]
    hit = jnp.any(expert_ids.T[:, None, :] == names[None], axis=0)
    weights = jnp.where(hit, jnp.exp(logits), 0.0)
    gates = weights / jnp.sum(weights, axis=0, keepdims=True)
    place = jnp.arange(tok_count, dtype=jnp.int32)
    earlier = (place[:, None] < place[None, :]).astype(jnp.bfloat16)
    slot = jnp.dot(hit.astype(jnp.bfloat16), earlier, preferred_element_type=jnp.float32)
    code = jnp.where(hit, slot + (half * capacity).astype(jnp.float32), -1.0)
    info = jnp.stack([gates.reshape(2, group, tok_count), code.reshape(2, group, tok_count)], axis=1)

    combined, slot_grads, router = layer(rows, down_weight[0], mixed_grad, info, gates, tokens)
    slot_grads = slot_grads.reshape(group, 2, capacity, slot_grads.shape[-1]).transpose(2, 1, 0, 3)
    row_grads = slot_grads.reshape(1, capacity, 1, sources, slot_grads.shape[-1])
    each = experts // dp_ranks
    router = router.reshape(dp_ranks, tp_ranks, each, -1, 128).transpose(0, 2, 1, 3, 4)
    router_grad = router.reshape(experts, tokens.shape[1]).T
    return (combined, row_grads, router_grad)


def solution(mesh):
    return jax.shard_map(
        per_device,
        mesh=mesh,
        in_specs=(
            P(("dp", "ctx"), None),
            P(),
            P("dp", None, "ctx", None, "tp"),
            P("ctx", "tp", None),
            P(("dp", "ctx"), None),
            P(("dp", "ctx"), None),
        ),
        out_specs=(P(("dp", "ctx"), "tp"), P("dp", None, "ctx", None, "tp"), P()),
        check_vma=False,
    )
```

```python
import jax
import jax.numpy as jnp
from jax import lax
from jax.experimental import pallas as pl
from jax.experimental.pallas import tpu as pltpu
from jax.sharding import PartitionSpec as P

MESH = pl.DeviceIdType.MESH
AHEAD = 3


def layer_kernel(
    rows_ref, weight_ref, grad_ref, ids_ref, router_ref, tok_ref,
    comb_ref, slot_grad_ref, out_ref,
    weight, grads, token_all, made, arrived, passed_in, passed_out, mix, chosen, dots, total,
    row_gate, info, info_out, gates, gg_out, gg_all, comb_out, comb_in, grad_out, part, from_dp, from_ctx,
    load_sem, tok_sem, weight_sem, x_send, x_recv, z_send, z_recv, mg_send, mg_recv,
    pair_send, pair_recv, rg_send, rg_recv, gg_send, gg_recv,
    send1, recv1, send2, recv2, send3, recv3, send4, recv4,
):
    dp, ctx, z = lax.axis_index("dp"), lax.axis_index("ctx"), lax.axis_index("tp")
    n_dp, n_ctx, n_z = lax.axis_size("dp"), lax.axis_size("ctx"), lax.axis_size("tp")
    n_q = n_ctx // 2
    half, q = ctx // n_q, lax.rem(ctx, n_q)
    last = n_z - 1
    cols = grads.shape[2]
    toks = grad_ref.shape[0]
    own_rows = pl.ds(pl.multiple_of(half * toks, toks), toks)
    other_rows = pl.ds(pl.multiple_of((1 - half) * toks, toks), toks)

    def at_dp(k):
        return (lax.rem(dp + k, n_dp), ctx, z)

    def at_ctx(k):
        return (dp, lax.rem(ctx + k, n_ctx), z)

    def at_z(k):
        return (dp, ctx, lax.rem(z + k, n_z))

    def at_q(k):
        return (dp, half * n_q + lax.rem(q + k, n_q), z)

    def remote(src, dst, send, recv, device):
        return pltpu.make_async_remote_copy(
            src_ref=src, dst_ref=dst, send_sem=send, recv_sem=recv, device_id=device, device_id_type=MESH
        )

    pair = (dp, (1 - half) * n_q + q, z)
    upper = (dp, ctx, jnp.minimum(z + 1, last))
    lower = (dp, ctx, jnp.maximum(z - 1, 0))

    flip = z // (n_z // 2)
    near = z + flip * (last - 2 * z)

    def block_at(n):
        later = n - (last - 2 * near)
        reach = near - later // 2
        inner = near + reach - 2 * reach * lax.rem(later + 2 * n_z, 2)
        block = jnp.where(later < 0, last - n, inner)
        return block + flip * (last - 2 * block)

    width = token_all.shape[1] // n_z
    tok_load = pltpu.make_async_copy(tok_ref, token_all, tok_sem)

    def weight_load(b):
        return pltpu.make_async_copy(
            weight_ref.at[:, pl.ds(pl.multiple_of(b * cols, 128), cols)], weight.at[b], weight_sem.at[b]
        )

    def grad_load(b):
        return pltpu.make_async_copy(
            grad_ref.at[:, pl.ds(pl.multiple_of(b * cols, 128), cols)], grads.at[b, own_rows], load_sem.at[b]
        )

    barrier = pltpu.get_barrier_semaphore()
    for count, where in ((n_z, at_z), (n_dp, at_dp), (n_ctx, at_ctx)):
        @pl.loop(1, count)
        def _(k):
            pl.semaphore_signal(barrier, inc=1, device_id=where(k), device_id_type=MESH)

    @pl.loop(1, n_z)
    def _(k):
        there = (dp, (1 - half) * n_q + q, lax.rem(z + k, n_z))
        pl.semaphore_signal(barrier, inc=1, device_id=there, device_id_type=MESH)

    @pl.loop(0, n_z)
    def _(n):
        weight_load(block_at(n)).start()

    tok_load.start()

    @pl.loop(0, n_z)
    def _(b):
        grad_load(b).start()

    def x_copy(b, k):
        to = lax.rem(q + k, n_q)
        return remote(made.at[b, to], arrived.at[b, q], x_send.at[b, to], x_recv.at[b, q], at_q(k))

    def x_wait(b, k):
        come = lax.rem(q + k, n_q)
        return remote(made.at[b, come], arrived.at[b, come], x_send.at[b, come], x_recv.at[b, come], at_q(k))

    def multiply(n):
        b = block_at(n)
        weight_load(b).wait()

        @pl.loop(0, n_q // 2)
        def _(r):
            rows = rows_ref[pl.ds(2 * r, 2)]
            size = rows.shape[1]
            product = jnp.dot(
                rows.reshape(2 * size, rows.shape[2]), weight[b], preferred_element_type=jnp.float32
            )
            made[b, pl.ds(2 * r, 2)] = product.astype(jnp.bfloat16).reshape(2, size, cols)

    def send(n):
        b = block_at(n)

        @pl.loop(1, n_q)
        def _(k):
            x_copy(b, k).start()

        arrived[b, q] = made[b, q]

    multiply(0)
    pl.semaphore_wait(barrier, 2 * n_z + n_dp + n_ctx - 4)
    send(0)

    tok_load.wait()
    logits = lax.dot_general(
        router_ref[...], token_all[...], (((1,), (1,)), ((), ())), preferred_element_type=jnp.float32
    )
    experts = logits.shape[0]
    names = lax.broadcasted_iota(jnp.int32, logits.shape, 0)
    hits = jnp.zeros(logits.shape, jnp.float32)
    for k in range(ids_ref.shape[0]):
        hits = jnp.where(jnp.broadcast_to(ids_ref[k : k + 1, :], names.shape) == names, 1.0, hits)
    hit = hits > 0.5
    weights = jnp.where(hit, jnp.exp(logits), 0.0)
    gate_values = weights / jnp.sum(weights, axis=0, keepdims=True)
    gates[...] = gate_values
    before = lax.broadcasted_iota(jnp.int32, (toks, toks), 0) < lax.broadcasted_iota(jnp.int32, (toks, toks), 1)
    slot = jnp.dot(
        hits.astype(jnp.bfloat16), jnp.where(before, 1.0, 0.0).astype(jnp.bfloat16), preferred_element_type=jnp.float32
    )
    capacity = rows_ref.shape[1] // 2
    code = jnp.where(hit, slot + (half * capacity).astype(jnp.float32), -1.0)
    for h in range(2):
        info_out[h, 0] = gate_values[h * n_q : (h + 1) * n_q]
        info_out[h, 1] = code[h * n_q : (h + 1) * n_q]
    info[half] = info_out[half]
    pair_info = remote(info_out.at[1 - half], info.at[half], pair_send.at[0], pair_recv.at[0], pair)
    pair_grad = remote(grads.at[z, own_rows], grads.at[z, own_rows], pair_send.at[1], pair_recv.at[1], pair)
    got_info = remote(info_out.at[half], info.at[1 - half], pair_send.at[0], pair_recv.at[0], pair)
    got_grad = remote(grads.at[z, other_rows], grads.at[z, other_rows], pair_send.at[1], pair_recv.at[1], pair)
    pair_info.start()

    for n in range(1, AHEAD):
        multiply(n)
        send(n)

    @pl.loop(0, n_z)
    def _(b):
        grad_load(b).wait()

    got_info.wait_recv()
    pair_grad.start()
    per_q = rows_ref.shape[1]
    experts_here = n_q

    def chosen_mask():
        code = jnp.concatenate([info[0, 1], info[1, 1]], axis=1)
        spot = lax.broadcasted_iota(jnp.int32, (experts_here, per_q, 2 * toks), 1).astype(jnp.float32)
        return jnp.broadcast_to(code[:, None, :], spot.shape) == spot

    mask = chosen_mask()
    gate = jnp.concatenate([info[0, 0], info[1, 0]], axis=1)
    spread = jnp.where(mask, jnp.broadcast_to(gate[:, None, :], mask.shape), 0.0)
    spread = spread.reshape(experts_here * per_q, 2 * toks)
    chosen[...] = jnp.where(mask, 1.0, 0.0).reshape(spread.shape).astype(jnp.bfloat16)
    turned = spread.T
    high = turned.astype(jnp.bfloat16)
    mix[0] = high
    mix[1] = (turned - high.astype(jnp.float32)).astype(jnp.bfloat16)
    row_gate[...] = jnp.broadcast_to(jnp.sum(spread, axis=1, keepdims=True), row_gate.shape)
    dots[...] = jnp.zeros(dots.shape, jnp.float32)

    def rg_copy(k):
        to = lax.rem(q + k, n_q)
        return remote(grad_out.at[to], slot_grad_ref.at[q], rg_send.at[to], rg_recv.at[q], at_q(k))

    def rg_wait(k):
        come = lax.rem(q + k, n_q)
        return remote(grad_out.at[come], slot_grad_ref.at[come], rg_send.at[come], rg_recv.at[come], at_q(k))

    def mg_copy(b, device):
        here = grads.at[b, other_rows]
        return remote(here, here, mg_send.at[b], mg_recv.at[b], device)

    def mg_copy_low(b, device):
        here = grads.at[b, other_rows]
        return remote(here, here, mg_send.at[n_z + b], mg_recv.at[b], device)

    def mg_step(j):
        below, above = z - j, z + j

        @pl.when((j > 0) & (below >= 0))
        def _():
            mg_copy(below, lower).wait_recv()

        @pl.when((j > 0) & (above <= last))
        def _():
            mg_copy(above, upper).wait_recv()

        @pl.when((below >= 0) & (z < last))
        def _():
            mg_copy(below, upper).start()

        @pl.when((above <= last) & (z > 0))
        def _():
            mg_copy_low(above, lower).start()

    def mg_finish(j):
        below, above = z - j, z + j

        @pl.when((below >= 0) & (z < last))
        def _():
            mg_copy(below, upper).wait_send()

        @pl.when((above <= last) & (z > 0))
        def _():
            mg_copy_low(above, lower).wait_send()

    def mixed(b):
        rows = arrived[b].reshape(n_q * per_q, cols)
        return jnp.dot(mix[0], rows, preferred_element_type=jnp.float32) + jnp.dot(
            mix[1], rows, preferred_element_type=jnp.float32
        )

    def add_dots(b):
        rows = arrived[b].reshape(n_q * per_q, cols)
        dots[...] += lax.dot_general(
            rows, grads[b], (((1,), (1,)), ((), ())), preferred_element_type=jnp.float32
        )

    def far_dots(n):
        @pl.when(z + n <= last)
        def _():
            add_dots(z + n)

        @pl.when(z - n >= 0)
        def _():
            add_dots(z - n)

    def z_copy(b, slot, s, device):
        span = pl.ds(s * toks, toks)
        return remote(
            passed_out.at[b, span], passed_in.at[slot, span], z_send.at[b, s], z_recv.at[slot, s], device
        )

    def x_wait_all(b):
        @pl.loop(1, n_q)
        def _(k):
            x_wait(b, k).wait_recv()

    @pl.loop(0, last)
    def _(n):
        b = block_at(n)
        x_wait_all(b)

        total[...] = mixed(b)
        up = b > z
        fed = (up & (z > 0)) | (jnp.logical_not(up) & (z < last))
        for s in range(2):
            span = pl.ds(s * toks, toks)

            @pl.when(fed)
            def _():
                z_copy(b, b, s, lower).wait_recv()
                total[span, :] += passed_in[b, span].astype(jnp.float32)

            passed_out[b, span] = total[span, :].astype(jnp.bfloat16)

            @pl.when(up)
            def _():
                z_copy(b, b, s, upper).start()

            @pl.when(b < z - 1)
            def _():
                z_copy(b, b, s, lower).start()

            @pl.when(b == z - 1)
            def _():
                z_copy(b, n_z, s, lower).start()

        @pl.when(n + AHEAD < n_z)
        def _():
            multiply(n + AHEAD)
            send(n + AHEAD)

        @pl.when(n == 0)
        def _():
            got_grad.wait_recv()
            picked_grad = jnp.dot(chosen[...], grads[z], preferred_element_type=jnp.float32)
            grad_out[...] = (picked_grad * row_gate[:, :1]).astype(jnp.bfloat16).reshape(grad_out.shape)
            slot_grad_ref[q] = grad_out[q]

        mg_step(n)

        @pl.when(n == n_z // 2)
        def _():
            @pl.loop(0, n_z // 2)
            def _(m):
                early = block_at(m)

                @pl.when((early - z <= n_z // 2) & (z - early <= n_z // 2))
                def _():
                    add_dots(early)

        @pl.when(n >= n_z // 2)
        def _():
            add_dots(b)

        @pl.when(n > n_z // 2)
        def _():
            far_dots(n)

    mg_step(last)
    far_dots(last)
    x_wait_all(z)
    add_dots(z)
    gate_grad = jnp.where(chosen_mask(), dots[...].reshape(experts_here, per_q, 2 * toks), 0.0)
    gate_grad = jnp.sum(gate_grad, axis=1)
    gg_out[0] = gate_grad[:, :toks]
    gg_out[1] = gate_grad[:, toks:]
    gg_all[half * n_z + z] = gg_out[half]
    spot = half * n_z + z

    def gg_copy(k, slot):
        to = lax.rem(spot + k, 2 * n_z)
        to_half = to // n_z
        return remote(
            gg_out.at[to_half], gg_all.at[slot], gg_send.at[to], gg_recv.at[slot],
            (dp, to_half * n_q + q, lax.rem(to, n_z)),
        )

    @pl.loop(1, 2 * n_z)
    def _(k):
        gg_copy(k, spot).start()

    @pl.loop(1, n_q)
    def _(k):
        rg_copy(k).start()

    total[...] = mixed(z)

    for s in range(2):
        span = pl.ds(s * toks, toks)

        @pl.when(z > 0)
        def _():
            z_copy(z, z, s, lower).wait_recv()
            total[span, :] += passed_in[z, span].astype(jnp.float32)

        @pl.when(z < last)
        def _():
            z_copy(z, n_z, s, upper).wait_recv()
            total[span, :] += passed_in[n_z, span].astype(jnp.float32)

    comb_out[...] = total[other_rows, :].astype(jnp.bfloat16)
    pair_comb = remote(comb_out, comb_in, pair_send.at[2], pair_recv.at[2], pair)
    @pl.loop(1, 2 * n_z)
    def _(k):
        gg_copy(k, lax.rem(spot + k, 2 * n_z)).wait_recv()

    parts = []
    for h in range(2):
        summed = gg_all[h * n_z]
        for k in range(1, n_z):
            summed = summed + gg_all[h * n_z + k]
        parts.append(summed)
    gate_grad = jnp.concatenate(parts, axis=0)
    gate_values = gates[...]
    mix_term = jnp.sum(gate_values * gate_grad, axis=0, keepdims=True)
    logit_grad = gate_values * (gate_grad - mix_term)
    high = logit_grad.astype(jnp.bfloat16)
    rest = logit_grad - high.astype(jnp.float32)
    middle = rest.astype(jnp.bfloat16)
    low = (rest - middle.astype(jnp.float32)).astype(jnp.bfloat16)
    token_cols = token_all[:, pl.ds(pl.multiple_of(z * width, 128), width)]
    product = jnp.dot(low, token_cols, preferred_element_type=jnp.float32)
    product += jnp.dot(middle, token_cols, preferred_element_type=jnp.float32)
    product += jnp.dot(high, token_cols, preferred_element_type=jnp.float32)
    product = product * (1.0 / toks)
    each, lanes = experts // n_dp, width // 128
    for e in range(experts):
        for k in range(lanes):
            row = (e % each) * lanes + k
            part[e // each, row // 4, row % 4 : row % 4 + 1, :] = product[e : e + 1, k * 128 : (k + 1) * 128]

    def exchange(count, me, where, source, target, send, recv):
        def copy(k, slot):
            to = lax.rem(me + k, count)
            return remote(source(to), target(slot), send.at[to], recv.at[slot], where(k))

        @pl.loop(1, count)
        def _(k):
            copy(k, me).start()

        @pl.loop(1, count)
        def _(k):
            copy(k, lax.rem(me + k, count)).wait_recv()

        @pl.loop(1, count)
        def _(k):
            copy(k, me).wait_send()

    from_dp[dp] = part[dp]
    exchange(n_dp, dp, at_dp, lambda k: part.at[k], lambda k: from_dp.at[k], send1, recv1)
    summed = from_dp[0]
    for k in range(1, n_dp):
        summed = summed + from_dp[k]
    from_ctx[ctx] = summed
    exchange(n_ctx, ctx, at_ctx, lambda k: from_ctx.at[ctx], lambda k: from_ctx.at[k], send2, recv2)
    summed = from_ctx[0]
    for k in range(1, n_ctx):
        summed = summed + from_ctx[k]
    out_ref[dp, z] = summed
    exchange(n_z, z, at_z, lambda k: out_ref.at[dp, z], lambda k: out_ref.at[dp, k], send3, recv3)
    pair_comb.start()
    exchange(n_dp, dp, at_dp, lambda k: out_ref.at[dp], lambda k: out_ref.at[k], send4, recv4)

    remote(comb_out, comb_in, pair_send.at[2], pair_recv.at[2], pair).wait_recv()
    comb_ref[...] = (total[own_rows, :] + comb_in[...].astype(jnp.float32)).astype(jnp.bfloat16)

    @pl.loop(1, n_q)
    def _(k):
        rg_wait(k).wait_recv()

    pair_info.wait_send()
    pair_grad.wait_send()
    pair_comb.wait_send()

    @pl.loop(1, n_q)
    def _(k):
        rg_copy(k).wait_send()

    @pl.loop(1, 2 * n_z)
    def _(k):
        gg_copy(k, spot).wait_send()

    @pl.loop(0, n_z)
    def _(j):
        mg_finish(j)

        @pl.loop(1, n_q)
        def _(k):
            x_copy(j, k).wait_send()

        @pl.when(j != z)
        def _():
            z_copy(j, j, 0, lower).wait_send()
            z_copy(j, j, 1, lower).wait_send()


def layer(rows, weight, grad, ids, router_weight, tokens):
    n_dp, n_ctx, n_z = lax.axis_size("dp"), lax.axis_size("ctx"), lax.axis_size("tp")
    n_q = n_ctx // 2
    per_q, depth = rows.shape[1:]
    full = weight.shape[1]
    cols = full // n_z
    experts, toks = router_weight.shape[0], tokens.shape[0]
    width = tokens.shape[1] // n_z
    each, lanes = experts // n_dp, width // 128
    chunk = (each * lanes // 4, 4, 128)
    vmem = pl.BlockSpec(memory_space=pltpu.VMEM)
    anywhere = pl.BlockSpec(memory_space=pl.ANY)
    bf16, f32 = jnp.bfloat16, jnp.float32
    dma = pltpu.SemaphoreType.DMA
    scratch = [
        pltpu.VMEM((n_z, depth, cols), bf16),
        pltpu.VMEM((n_z, 2 * toks, cols), bf16),
        pltpu.VMEM(tokens.shape, bf16),
        pltpu.VMEM((n_z, n_q, per_q, cols), bf16),
        pltpu.VMEM((n_z, n_q, per_q, cols), bf16),
        pltpu.VMEM((n_z + 1, 2 * toks, cols), bf16),
        pltpu.VMEM((n_z, 2 * toks, cols), bf16),
        pltpu.VMEM((2, 2 * toks, n_q * per_q), bf16),
        pltpu.VMEM((n_q * per_q, 2 * toks), bf16),
        pltpu.VMEM((n_q * per_q, 2 * toks), f32),
        pltpu.VMEM((2 * toks, cols), f32),
        pltpu.VMEM((n_q * per_q, 128), f32),
        pltpu.VMEM((2, 2, n_q, toks), f32),
        pltpu.VMEM((2, 2, n_q, toks), f32),
        pltpu.VMEM((experts, toks), f32),
        pltpu.VMEM((2, n_q, toks), f32),
        pltpu.VMEM((2 * n_z, n_q, toks), f32),
        pltpu.VMEM((toks, cols), bf16),
        pltpu.VMEM((toks, cols), bf16),
        pltpu.VMEM((n_q, per_q, cols), bf16),
        pltpu.VMEM((n_dp,) + chunk, f32),
        pltpu.VMEM((n_dp,) + chunk, f32),
        pltpu.VMEM((n_ctx,) + chunk, f32),
        dma((n_z,)), dma, dma((n_z,)),
        dma((n_z, n_q)), dma((n_z, n_q)),
        dma((n_z, 2)), dma((n_z + 1, 2)),
        dma((2 * n_z,)), dma((n_z,)),
        dma((3,)), dma((3,)),
        dma((n_q,)), dma((n_q,)),
        dma((2 * n_z,)), dma((2 * n_z,)),
        dma((n_dp,)), dma((n_dp,)), dma((n_ctx,)), dma((n_ctx,)),
        dma((n_z,)), dma((n_z,)), dma((n_dp,)), dma((n_dp,)),
    ]
    return pl.pallas_call(
        layer_kernel,
        out_shape=(
            jax.ShapeDtypeStruct((toks, cols), bf16),
            jax.ShapeDtypeStruct((n_q, per_q, cols), bf16),
            jax.ShapeDtypeStruct((n_dp, n_z) + chunk, f32),
        ),
        in_specs=[vmem, anywhere, anywhere, vmem, vmem, anywhere],
        out_specs=(vmem, vmem, vmem),
        scratch_shapes=scratch,
        compiler_params=pltpu.CompilerParams(collective_id=1, has_side_effects=True, vmem_limit_bytes=56 << 20),
        name="layer",
    )(rows, weight, grad, ids, router_weight, tokens)


def per_device(tokens, router_weight, expert_hidden, down_weight, expert_ids, mixed_grad):
    tp_ranks, dp_ranks = lax.axis_size("tp"), lax.axis_size("dp")
    hidden = expert_hidden[0, :, 0]
    capacity, sources, depth = hidden.shape
    experts = router_weight.shape[1]
    group = sources // 2
    rows = hidden.reshape(capacity, 2, group, depth).transpose(2, 1, 0, 3)
    rows = rows.reshape(group, 2 * capacity, depth)

    combined, slot_grads, router = layer(
        rows, down_weight[0], mixed_grad, expert_ids.T, router_weight.T, tokens
    )
    slot_grads = slot_grads.reshape(group, 2, capacity, slot_grads.shape[-1]).transpose(2, 1, 0, 3)
    row_grads = slot_grads.reshape(1, capacity, 1, sources, slot_grads.shape[-1])
    each = experts // dp_ranks
    router = router.reshape(dp_ranks, tp_ranks, each, -1, 128).transpose(0, 2, 1, 3, 4)
    router_grad = router.reshape(experts, tokens.shape[1]).T
    return (combined, row_grads, router_grad)


def solution(mesh):
    return jax.shard_map(
        per_device,
        mesh=mesh,
        in_specs=(
            P(("dp", "ctx"), None),
            P(),
            P("dp", None, "ctx", None, "tp"),
            P("ctx", "tp", None),
            P(("dp", "ctx"), None),
            P(("dp", "ctx"), None),
        ),
        out_specs=(P(("dp", "ctx"), "tp"), P("dp", None, "ctx", None, "tp"), P()),
        check_vma=False,
    )
```

```python
import jax
import jax.numpy as jnp
from jax import lax
from jax.experimental import pallas as pl
from jax.experimental.pallas import tpu as pltpu
from jax.sharding import PartitionSpec as P

MESH = pl.DeviceIdType.MESH
AHEAD = 3


def layer_kernel(
    rows_ref, weight_ref, grad_ref, ids_ref, router_ref, tok_ref,
    comb_ref, slot_grad_ref, out_ref,
    weight, grads, token_all, made, arrived, passed_in, passed_out, mix, chosen, dots, total,
    row_gate, info, info_out, gates, gg_out, gg_all, comb_out, comb_in, grad_out, part, from_dp, from_ctx,
    load_sem, tok_sem, weight_sem, x_send, x_recv, z_send, z_recv, mg_send, mg_recv,
    pair_send, pair_recv, rg_send, rg_recv, gg_send, gg_recv,
    send1, recv1, send2, recv2, send3, recv3, send4, recv4,
):
    dp, ctx, z = lax.axis_index("dp"), lax.axis_index("ctx"), lax.axis_index("tp")
    n_dp, n_ctx, n_z = lax.axis_size("dp"), lax.axis_size("ctx"), lax.axis_size("tp")
    n_q = n_ctx // 2
    half, q = ctx // n_q, lax.rem(ctx, n_q)
    last = n_z - 1
    cols = grads.shape[2]
    toks = grad_ref.shape[0]
    own_rows = pl.ds(pl.multiple_of(half * toks, toks), toks)
    other_rows = pl.ds(pl.multiple_of((1 - half) * toks, toks), toks)

    def at_dp(k):
        return (lax.rem(dp + k, n_dp), ctx, z)

    def at_ctx(k):
        return (dp, lax.rem(ctx + k, n_ctx), z)

    def at_z(k):
        return (dp, ctx, lax.rem(z + k, n_z))

    def at_q(k):
        return (dp, half * n_q + lax.rem(q + k, n_q), z)

    def remote(src, dst, send, recv, device):
        return pltpu.make_async_remote_copy(
            src_ref=src, dst_ref=dst, send_sem=send, recv_sem=recv, device_id=device, device_id_type=MESH
        )

    pair = (dp, (1 - half) * n_q + q, z)
    upper = (dp, ctx, jnp.minimum(z + 1, last))
    lower = (dp, ctx, jnp.maximum(z - 1, 0))

    flip = z // (n_z // 2)
    near = z + flip * (last - 2 * z)

    def block_at(n):
        later = n - (last - 2 * near)
        reach = near - later // 2
        inner = near + reach - 2 * reach * lax.rem(later + 2 * n_z, 2)
        block = jnp.where(later < 0, last - n, inner)
        return block + flip * (last - 2 * block)

    width = token_all.shape[1] // n_z
    tok_load = pltpu.make_async_copy(tok_ref, token_all, tok_sem)

    def weight_load(b):
        return pltpu.make_async_copy(
            weight_ref.at[:, pl.ds(pl.multiple_of(b * cols, 128), cols)], weight.at[b], weight_sem.at[b]
        )

    def grad_load(b):
        return pltpu.make_async_copy(
            grad_ref.at[:, pl.ds(pl.multiple_of(b * cols, 128), cols)], grads.at[b, own_rows], load_sem.at[b]
        )

    barrier = pltpu.get_barrier_semaphore()
    for count, where in ((n_z, at_z), (n_dp, at_dp), (n_ctx, at_ctx)):
        @pl.loop(1, count)
        def _(k):
            pl.semaphore_signal(barrier, inc=1, device_id=where(k), device_id_type=MESH)

    @pl.loop(1, n_z)
    def _(k):
        there = (dp, (1 - half) * n_q + q, lax.rem(z + k, n_z))
        pl.semaphore_signal(barrier, inc=1, device_id=there, device_id_type=MESH)

    @pl.loop(0, n_z)
    def _(n):
        weight_load(block_at(n)).start()

    tok_load.start()

    @pl.loop(0, n_z)
    def _(b):
        grad_load(b).start()

    def x_copy(b, k):
        to = lax.rem(q + k, n_q)
        return remote(made.at[b, to], arrived.at[b, q], x_send.at[b, to], x_recv.at[b, q], at_q(k))

    def x_wait(b, k):
        come = lax.rem(q + k, n_q)
        return remote(made.at[b, come], arrived.at[b, come], x_send.at[b, come], x_recv.at[b, come], at_q(k))

    def multiply(n):
        b = block_at(n)
        weight_load(b).wait()

        @pl.loop(0, n_q // 2)
        def _(r):
            rows = rows_ref[pl.ds(2 * r, 2)]
            size = rows.shape[1]
            product = jnp.dot(
                rows.reshape(2 * size, rows.shape[2]), weight[b], preferred_element_type=jnp.float32
            )
            made[b, pl.ds(2 * r, 2)] = product.astype(jnp.bfloat16).reshape(2, size, cols)

    def send(n):
        b = block_at(n)

        @pl.loop(1, n_q)
        def _(k):
            x_copy(b, k).start()

        arrived[b, q] = made[b, q]

    multiply(0)
    pl.semaphore_wait(barrier, 2 * n_z + n_dp + n_ctx - 4)
    send(0)

    tok_load.wait()
    logits = lax.dot_general(
        router_ref[...], token_all[...], (((1,), (1,)), ((), ())), preferred_element_type=jnp.float32
    )
    experts = logits.shape[0]
    names = lax.broadcasted_iota(jnp.int32, logits.shape, 0)
    hits = jnp.zeros(logits.shape, jnp.float32)
    for k in range(ids_ref.shape[0]):
        hits = jnp.where(jnp.broadcast_to(ids_ref[k : k + 1, :], names.shape) == names, 1.0, hits)
    hit = hits > 0.5
    weights = jnp.where(hit, jnp.exp(logits), 0.0)
    gate_values = weights / jnp.sum(weights, axis=0, keepdims=True)
    gates[...] = gate_values
    before = lax.broadcasted_iota(jnp.int32, (toks, toks), 0) < lax.broadcasted_iota(jnp.int32, (toks, toks), 1)
    slot = jnp.dot(
        hits.astype(jnp.bfloat16), jnp.where(before, 1.0, 0.0).astype(jnp.bfloat16), preferred_element_type=jnp.float32
    )
    capacity = rows_ref.shape[1] // 2
    code = jnp.where(hit, slot + (half * capacity).astype(jnp.float32), -1.0)
    for h in range(2):
        info_out[h, 0] = gate_values[h * n_q : (h + 1) * n_q]
        info_out[h, 1] = code[h * n_q : (h + 1) * n_q]
    info[half] = info_out[half]
    pair_info = remote(info_out.at[1 - half], info.at[half], pair_send.at[0], pair_recv.at[0], pair)
    pair_grad = remote(grads.at[z, own_rows], grads.at[z, own_rows], pair_send.at[1], pair_recv.at[1], pair)
    got_info = remote(info_out.at[half], info.at[1 - half], pair_send.at[0], pair_recv.at[0], pair)
    got_grad = remote(grads.at[z, other_rows], grads.at[z, other_rows], pair_send.at[1], pair_recv.at[1], pair)
    pair_info.start()

    for n in range(1, AHEAD):
        multiply(n)
        send(n)

    @pl.loop(0, n_z)
    def _(b):
        grad_load(b).wait()

    got_info.wait_recv()
    pair_grad.start()
    per_q = rows_ref.shape[1]
    experts_here = n_q

    def chosen_mask():
        code = jnp.concatenate([info[0, 1], info[1, 1]], axis=1)
        spot = lax.broadcasted_iota(jnp.int32, (experts_here, per_q, 2 * toks), 1).astype(jnp.float32)
        return jnp.broadcast_to(code[:, None, :], spot.shape) == spot

    mask = chosen_mask()
    gate = jnp.concatenate([info[0, 0], info[1, 0]], axis=1)
    spread = jnp.where(mask, jnp.broadcast_to(gate[:, None, :], mask.shape), 0.0)
    spread = spread.reshape(experts_here * per_q, 2 * toks)
    chosen[...] = jnp.where(mask, 1.0, 0.0).reshape(spread.shape).astype(jnp.bfloat16)
    turned = spread.T
    high = turned.astype(jnp.bfloat16)
    mix[0] = high
    mix[1] = (turned - high.astype(jnp.float32)).astype(jnp.bfloat16)
    row_gate[...] = jnp.broadcast_to(jnp.sum(spread, axis=1, keepdims=True), row_gate.shape)
    dots[...] = jnp.zeros(dots.shape, jnp.float32)

    def rg_copy(k):
        to = lax.rem(q + k, n_q)
        return remote(grad_out.at[to], slot_grad_ref.at[q], rg_send.at[to], rg_recv.at[q], at_q(k))

    def rg_wait(k):
        come = lax.rem(q + k, n_q)
        return remote(grad_out.at[come], slot_grad_ref.at[come], rg_send.at[come], rg_recv.at[come], at_q(k))

    def mg_copy(b, device):
        here = grads.at[b, other_rows]
        return remote(here, here, mg_send.at[b], mg_recv.at[b], device)

    def mg_copy_low(b, device):
        here = grads.at[b, other_rows]
        return remote(here, here, mg_send.at[n_z + b], mg_recv.at[b], device)

    def mg_step(j):
        below, above = z - j, z + j

        @pl.when((j > 0) & (below >= 0))
        def _():
            mg_copy(below, lower).wait_recv()

        @pl.when((j > 0) & (above <= last))
        def _():
            mg_copy(above, upper).wait_recv()

        @pl.when((below >= 0) & (z < last))
        def _():
            mg_copy(below, upper).start()

        @pl.when((above <= last) & (z > 0))
        def _():
            mg_copy_low(above, lower).start()

    def mg_finish(j):
        below, above = z - j, z + j

        @pl.when((below >= 0) & (z < last))
        def _():
            mg_copy(below, upper).wait_send()

        @pl.when((above <= last) & (z > 0))
        def _():
            mg_copy_low(above, lower).wait_send()

    def mixed(b):
        rows = arrived[b].reshape(n_q * per_q, cols)
        return jnp.dot(mix[0], rows, preferred_element_type=jnp.float32) + jnp.dot(
            mix[1], rows, preferred_element_type=jnp.float32
        )

    def add_dots(b):
        rows = arrived[b].reshape(n_q * per_q, cols)
        dots[...] += lax.dot_general(
            rows, grads[b], (((1,), (1,)), ((), ())), preferred_element_type=jnp.float32
        )

    def far_dots(n):
        @pl.when(z + n <= last)
        def _():
            add_dots(z + n)

        @pl.when(z - n >= 0)
        def _():
            add_dots(z - n)

    def z_copy(b, slot, s, device):
        span = pl.ds(s * toks, toks)
        return remote(
            passed_out.at[b, span], passed_in.at[slot, span], z_send.at[b, s], z_recv.at[slot, s], device
        )

    def x_wait_all(b):
        @pl.loop(1, n_q)
        def _(k):
            x_wait(b, k).wait_recv()

    def pass_on(n):
        b = block_at(n)
        total[...] = mixed(b)
        up = b > z
        fed = (up & (z > 0)) | (jnp.logical_not(up) & (z < last))
        for s in range(2):
            span = pl.ds(s * toks, toks)

            @pl.when(fed)
            def _():
                z_copy(b, b, s, lower).wait_recv()
                total[span, :] += passed_in[b, span].astype(jnp.float32)

            passed_out[b, span] = total[span, :].astype(jnp.bfloat16)

            @pl.when(up)
            def _():
                z_copy(b, b, s, upper).start()

            @pl.when(b < z - 1)
            def _():
                z_copy(b, b, s, lower).start()

            @pl.when(b == z - 1)
            def _():
                z_copy(b, n_z, s, lower).start()

    def gather_dots(n, b):
        mg_step(n)

        @pl.when(n == n_z // 2)
        def _():
            @pl.loop(0, n_z // 2)
            def _(m):
                early = block_at(m)

                @pl.when((early - z <= n_z // 2) & (z - early <= n_z // 2))
                def _():
                    add_dots(early)

        @pl.when(n >= n_z // 2)
        def _():
            add_dots(b)

        @pl.when(n > n_z // 2)
        def _():
            far_dots(n)

    @pl.loop(0, last)
    def _(n):
        b = block_at(n)
        x_wait_all(b)

        @pl.when(n + AHEAD < n_z)
        def _():
            multiply(n + AHEAD)
            send(n + AHEAD)

        @pl.when(n == 0)
        def _():
            got_grad.wait_recv()
            picked_grad = jnp.dot(chosen[...], grads[z], preferred_element_type=jnp.float32)
            grad_out[...] = (picked_grad * row_gate[:, :1]).astype(jnp.bfloat16).reshape(grad_out.shape)
            slot_grad_ref[q] = grad_out[q]

        gather_dots(n, b)

        @pl.when(n > 0)
        def _():
            pass_on(n - 1)

    mg_step(last)
    far_dots(last)
    x_wait_all(z)
    add_dots(z)
    gate_grad = jnp.where(chosen_mask(), dots[...].reshape(experts_here, per_q, 2 * toks), 0.0)
    gate_grad = jnp.sum(gate_grad, axis=1)
    gg_out[0] = gate_grad[:, :toks]
    gg_out[1] = gate_grad[:, toks:]
    gg_all[half * n_z + z] = gg_out[half]
    spot = half * n_z + z

    def gg_copy(k, slot):
        to = lax.rem(spot + k, 2 * n_z)
        to_half = to // n_z
        return remote(
            gg_out.at[to_half], gg_all.at[slot], gg_send.at[to], gg_recv.at[slot],
            (dp, to_half * n_q + q, lax.rem(to, n_z)),
        )

    @pl.loop(1, 2 * n_z)
    def _(k):
        gg_copy(k, spot).start()

    @pl.loop(1, n_q)
    def _(k):
        rg_copy(k).start()

    pass_on(last - 1)

    @pl.loop(1, 2 * n_z)
    def _(k):
        gg_copy(k, lax.rem(spot + k, 2 * n_z)).wait_recv()

    parts = []
    for h in range(2):
        summed = gg_all[h * n_z]
        for k in range(1, n_z):
            summed = summed + gg_all[h * n_z + k]
        parts.append(summed)
    gate_grad = jnp.concatenate(parts, axis=0)
    gate_values = gates[...]
    mix_term = jnp.sum(gate_values * gate_grad, axis=0, keepdims=True)
    logit_grad = gate_values * (gate_grad - mix_term)
    high = logit_grad.astype(jnp.bfloat16)
    rest = logit_grad - high.astype(jnp.float32)
    middle = rest.astype(jnp.bfloat16)
    low = (rest - middle.astype(jnp.float32)).astype(jnp.bfloat16)
    token_cols = token_all[:, pl.ds(pl.multiple_of(z * width, 128), width)]
    product = jnp.dot(low, token_cols, preferred_element_type=jnp.float32)
    product += jnp.dot(middle, token_cols, preferred_element_type=jnp.float32)
    product += jnp.dot(high, token_cols, preferred_element_type=jnp.float32)
    product = product * (1.0 / toks)
    each, lanes = experts // n_dp, width // 128
    for e in range(experts):
        for k in range(lanes):
            row = (e % each) * lanes + k
            part[e // each, row // 4, row % 4 : row % 4 + 1, :] = product[e : e + 1, k * 128 : (k + 1) * 128]

    pair_comb = remote(comb_out, comb_in, pair_send.at[2], pair_recv.at[2], pair)

    def finish_own():
        total[...] = mixed(z)

        for s in range(2):
            span = pl.ds(s * toks, toks)

            @pl.when(z > 0)
            def _():
                z_copy(z, z, s, lower).wait_recv()
                total[span, :] += passed_in[z, span].astype(jnp.float32)

            @pl.when(z < last)
            def _():
                z_copy(z, n_z, s, upper).wait_recv()
                total[span, :] += passed_in[n_z, span].astype(jnp.float32)

        comb_out[...] = total[other_rows, :].astype(jnp.bfloat16)
        pair_comb.start()

    def exchange(count, me, where, source, target, send, recv, meanwhile=None):
        def copy(k, slot):
            to = lax.rem(me + k, count)
            return remote(source(to), target(slot), send.at[to], recv.at[slot], where(k))

        @pl.loop(1, count)
        def _(k):
            copy(k, me).start()

        if meanwhile is not None:
            meanwhile()

        @pl.loop(1, count)
        def _(k):
            copy(k, lax.rem(me + k, count)).wait_recv()

        @pl.loop(1, count)
        def _(k):
            copy(k, me).wait_send()

    from_dp[dp] = part[dp]
    exchange(n_dp, dp, at_dp, lambda k: part.at[k], lambda k: from_dp.at[k], send1, recv1)
    summed = from_dp[0]
    for k in range(1, n_dp):
        summed = summed + from_dp[k]
    from_ctx[ctx] = summed
    exchange(n_ctx, ctx, at_ctx, lambda k: from_ctx.at[ctx], lambda k: from_ctx.at[k], send2, recv2, finish_own)
    summed = from_ctx[0]
    for k in range(1, n_ctx):
        summed = summed + from_ctx[k]
    out_ref[dp, z] = summed
    exchange(n_z, z, at_z, lambda k: out_ref.at[dp, z], lambda k: out_ref.at[dp, k], send3, recv3)
    exchange(n_dp, dp, at_dp, lambda k: out_ref.at[dp], lambda k: out_ref.at[k], send4, recv4)

    remote(comb_out, comb_in, pair_send.at[2], pair_recv.at[2], pair).wait_recv()
    comb_ref[...] = (total[own_rows, :] + comb_in[...].astype(jnp.float32)).astype(jnp.bfloat16)

    @pl.loop(1, n_q)
    def _(k):
        rg_wait(k).wait_recv()

    pair_info.wait_send()
    pair_grad.wait_send()
    pair_comb.wait_send()

    @pl.loop(1, n_q)
    def _(k):
        rg_copy(k).wait_send()

    @pl.loop(1, 2 * n_z)
    def _(k):
        gg_copy(k, spot).wait_send()

    @pl.loop(0, n_z)
    def _(j):
        mg_finish(j)

        @pl.loop(1, n_q)
        def _(k):
            x_copy(j, k).wait_send()

        @pl.when(j != z)
        def _():
            z_copy(j, j, 0, lower).wait_send()
            z_copy(j, j, 1, lower).wait_send()


def layer(rows, weight, grad, ids, router_weight, tokens):
    n_dp, n_ctx, n_z = lax.axis_size("dp"), lax.axis_size("ctx"), lax.axis_size("tp")
    n_q = n_ctx // 2
    per_q, depth = rows.shape[1:]
    full = weight.shape[1]
    cols = full // n_z
    experts, toks = router_weight.shape[0], tokens.shape[0]
    width = tokens.shape[1] // n_z
    each, lanes = experts // n_dp, width // 128
    chunk = (each * lanes // 4, 4, 128)
    vmem = pl.BlockSpec(memory_space=pltpu.VMEM)
    anywhere = pl.BlockSpec(memory_space=pl.ANY)
    bf16, f32 = jnp.bfloat16, jnp.float32
    dma = pltpu.SemaphoreType.DMA
    scratch = [
        pltpu.VMEM((n_z, depth, cols), bf16),
        pltpu.VMEM((n_z, 2 * toks, cols), bf16),
        pltpu.VMEM(tokens.shape, bf16),
        pltpu.VMEM((n_z, n_q, per_q, cols), bf16),
        pltpu.VMEM((n_z, n_q, per_q, cols), bf16),
        pltpu.VMEM((n_z + 1, 2 * toks, cols), bf16),
        pltpu.VMEM((n_z, 2 * toks, cols), bf16),
        pltpu.VMEM((2, 2 * toks, n_q * per_q), bf16),
        pltpu.VMEM((n_q * per_q, 2 * toks), bf16),
        pltpu.VMEM((n_q * per_q, 2 * toks), f32),
        pltpu.VMEM((2 * toks, cols), f32),
        pltpu.VMEM((n_q * per_q, 128), f32),
        pltpu.VMEM((2, 2, n_q, toks), f32),
        pltpu.VMEM((2, 2, n_q, toks), f32),
        pltpu.VMEM((experts, toks), f32),
        pltpu.VMEM((2, n_q, toks), f32),
        pltpu.VMEM((2 * n_z, n_q, toks), f32),
        pltpu.VMEM((toks, cols), bf16),
        pltpu.VMEM((toks, cols), bf16),
        pltpu.VMEM((n_q, per_q, cols), bf16),
        pltpu.VMEM((n_dp,) + chunk, f32),
        pltpu.VMEM((n_dp,) + chunk, f32),
        pltpu.VMEM((n_ctx,) + chunk, f32),
        dma((n_z,)), dma, dma((n_z,)),
        dma((n_z, n_q)), dma((n_z, n_q)),
        dma((n_z, 2)), dma((n_z + 1, 2)),
        dma((2 * n_z,)), dma((n_z,)),
        dma((3,)), dma((3,)),
        dma((n_q,)), dma((n_q,)),
        dma((2 * n_z,)), dma((2 * n_z,)),
        dma((n_dp,)), dma((n_dp,)), dma((n_ctx,)), dma((n_ctx,)),
        dma((n_z,)), dma((n_z,)), dma((n_dp,)), dma((n_dp,)),
    ]
    return pl.pallas_call(
        layer_kernel,
        out_shape=(
            jax.ShapeDtypeStruct((toks, cols), bf16),
            jax.ShapeDtypeStruct((n_q, per_q, cols), bf16),
            jax.ShapeDtypeStruct((n_dp, n_z) + chunk, f32),
        ),
        in_specs=[vmem, anywhere, anywhere, vmem, vmem, anywhere],
        out_specs=(vmem, vmem, vmem),
        scratch_shapes=scratch,
        compiler_params=pltpu.CompilerParams(collective_id=1, has_side_effects=True, vmem_limit_bytes=56 << 20),
        name="layer",
    )(rows, weight, grad, ids, router_weight, tokens)


def per_device(tokens, router_weight, expert_hidden, down_weight, expert_ids, mixed_grad):
    tp_ranks, dp_ranks = lax.axis_size("tp"), lax.axis_size("dp")
    hidden = expert_hidden[0, :, 0]
    capacity, sources, depth = hidden.shape
    experts = router_weight.shape[1]
    group = sources // 2
    rows = hidden.reshape(capacity, 2, group, depth).transpose(2, 1, 0, 3)
    rows = rows.reshape(group, 2 * capacity, depth)

    combined, slot_grads, router = layer(
        rows, down_weight[0], mixed_grad, expert_ids.T, router_weight.T, tokens
    )
    slot_grads = slot_grads.reshape(group, 2, capacity, slot_grads.shape[-1]).transpose(2, 1, 0, 3)
    row_grads = slot_grads.reshape(1, capacity, 1, sources, slot_grads.shape[-1])
    each = experts // dp_ranks
    router = router.reshape(dp_ranks, tp_ranks, each, -1, 128).transpose(0, 2, 1, 3, 4)
    router_grad = router.reshape(experts, tokens.shape[1]).T
    return (combined, row_grads, router_grad)


def solution(mesh):
    return jax.shard_map(
        per_device,
        mesh=mesh,
        in_specs=(
            P(("dp", "ctx"), None),
            P(),
            P("dp", None, "ctx", None, "tp"),
            P("ctx", "tp", None),
            P(("dp", "ctx"), None),
            P(("dp", "ctx"), None),
        ),
        out_specs=(P(("dp", "ctx"), "tp"), P("dp", None, "ctx", None, "tp"), P()),
        check_vma=False,
    )
```

```python
import jax
import jax.numpy as jnp
from jax import lax
from jax.experimental import pallas as pl
from jax.experimental.pallas import tpu as pltpu
from jax.sharding import PartitionSpec as P

MESH = pl.DeviceIdType.MESH
AHEAD = 3


def layer_kernel(
    rows_ref, weight_ref, grad_ref, ids_ref, router_ref, tok_ref,
    comb_ref, slot_grad_ref, out_ref,
    weight, grads, token_all, made, arrived, passed_in, passed_out, mix, chosen, dots, total,
    row_gate, info, info_out, gates, gg_out, gg_all, comb_out, comb_in, grad_out, part, from_dp, from_ctx, packed,
    load_sem, tok_sem, weight_sem, x_send, x_recv, z_send, z_recv, mg_send, mg_recv,
    pair_send, pair_recv, rg_send, rg_recv, gg_send, gg_recv,
    send1, recv1, send2, recv2, send3, recv3, send4, recv4,
):
    dp, ctx, z = lax.axis_index("dp"), lax.axis_index("ctx"), lax.axis_index("tp")
    n_dp, n_ctx, n_z = lax.axis_size("dp"), lax.axis_size("ctx"), lax.axis_size("tp")
    n_q = n_ctx // 2
    half, q = ctx // n_q, lax.rem(ctx, n_q)
    last = n_z - 1
    cols = grads.shape[2]
    toks = grad_ref.shape[0]
    own_rows = pl.ds(pl.multiple_of(half * toks, toks), toks)
    other_rows = pl.ds(pl.multiple_of((1 - half) * toks, toks), toks)

    def at_dp(k):
        return (lax.rem(dp + k, n_dp), ctx, z)

    def at_ctx(k):
        return (dp, lax.rem(ctx + k, n_ctx), z)

    def at_z(k):
        return (dp, ctx, lax.rem(z + k, n_z))

    def at_q(k):
        return (dp, half * n_q + lax.rem(q + k, n_q), z)

    def remote(src, dst, send, recv, device):
        return pltpu.make_async_remote_copy(
            src_ref=src, dst_ref=dst, send_sem=send, recv_sem=recv, device_id=device, device_id_type=MESH
        )

    pair = (dp, (1 - half) * n_q + q, z)
    upper = (dp, ctx, jnp.minimum(z + 1, last))
    lower = (dp, ctx, jnp.maximum(z - 1, 0))

    flip = z // (n_z // 2)
    near = z + flip * (last - 2 * z)

    def block_at(n):
        later = n - (last - 2 * near)
        reach = near - later // 2
        inner = near + reach - 2 * reach * lax.rem(later + 2 * n_z, 2)
        block = jnp.where(later < 0, last - n, inner)
        return block + flip * (last - 2 * block)

    width = token_all.shape[1] // n_z
    tok_load = pltpu.make_async_copy(tok_ref, token_all, tok_sem)

    def weight_load(b):
        return pltpu.make_async_copy(
            weight_ref.at[:, pl.ds(pl.multiple_of(b * cols, 128), cols)], weight.at[b], weight_sem.at[b]
        )

    def grad_load(b):
        return pltpu.make_async_copy(
            grad_ref.at[:, pl.ds(pl.multiple_of(b * cols, 128), cols)], grads.at[b, own_rows], load_sem.at[b]
        )

    barrier = pltpu.get_barrier_semaphore()
    for count, where in ((n_z, at_z), (n_dp, at_dp), (n_ctx, at_ctx)):
        @pl.loop(1, count)
        def _(k):
            pl.semaphore_signal(barrier, inc=1, device_id=where(k), device_id_type=MESH)

    @pl.loop(1, n_z)
    def _(k):
        there = (dp, (1 - half) * n_q + q, lax.rem(z + k, n_z))
        pl.semaphore_signal(barrier, inc=1, device_id=there, device_id_type=MESH)

    @pl.loop(0, n_z)
    def _(n):
        weight_load(block_at(n)).start()

    tok_load.start()

    @pl.loop(0, n_z)
    def _(b):
        grad_load(b).start()

    def x_copy(b, k):
        to = lax.rem(q + k, n_q)
        return remote(made.at[b, to], arrived.at[b, q], x_send.at[b, to], x_recv.at[b, q], at_q(k))

    def x_wait(b, k):
        come = lax.rem(q + k, n_q)
        return remote(made.at[b, come], arrived.at[b, come], x_send.at[b, come], x_recv.at[b, come], at_q(k))

    def multiply(n):
        b = block_at(n)
        weight_load(b).wait()

        @pl.loop(0, n_q // 2)
        def _(r):
            rows = rows_ref[pl.ds(2 * r, 2)]
            size = rows.shape[1]
            product = jnp.dot(
                rows.reshape(2 * size, rows.shape[2]), weight[b], preferred_element_type=jnp.float32
            )
            made[b, pl.ds(2 * r, 2)] = product.astype(jnp.bfloat16).reshape(2, size, cols)

    def send(n):
        b = block_at(n)

        @pl.loop(1, n_q)
        def _(k):
            x_copy(b, k).start()

        arrived[b, q] = made[b, q]

    multiply(0)
    pl.semaphore_wait(barrier, 2 * n_z + n_dp + n_ctx - 4)
    send(0)

    tok_load.wait()
    logits = lax.dot_general(
        router_ref[...], token_all[...], (((1,), (1,)), ((), ())), preferred_element_type=jnp.float32
    )
    experts = logits.shape[0]
    names = lax.broadcasted_iota(jnp.int32, logits.shape, 0)
    hits = jnp.zeros(logits.shape, jnp.float32)
    for k in range(ids_ref.shape[0]):
        hits = jnp.where(jnp.broadcast_to(ids_ref[k : k + 1, :], names.shape) == names, 1.0, hits)
    hit = hits > 0.5
    weights = jnp.where(hit, jnp.exp(logits), 0.0)
    gate_values = weights / jnp.sum(weights, axis=0, keepdims=True)
    gates[...] = gate_values
    before = lax.broadcasted_iota(jnp.int32, (toks, toks), 0) < lax.broadcasted_iota(jnp.int32, (toks, toks), 1)
    slot = jnp.dot(
        hits.astype(jnp.bfloat16), jnp.where(before, 1.0, 0.0).astype(jnp.bfloat16), preferred_element_type=jnp.float32
    )
    capacity = rows_ref.shape[1] // 2
    code = jnp.where(hit, slot + (half * capacity).astype(jnp.float32), -1.0)
    for h in range(2):
        info_out[h, 0] = gate_values[h * n_q : (h + 1) * n_q]
        info_out[h, 1] = code[h * n_q : (h + 1) * n_q]
    info[half] = info_out[half]
    pair_info = remote(info_out.at[1 - half], info.at[half], pair_send.at[0], pair_recv.at[0], pair)
    pair_grad = remote(grads.at[z, own_rows], grads.at[z, own_rows], pair_send.at[1], pair_recv.at[1], pair)
    got_info = remote(info_out.at[half], info.at[1 - half], pair_send.at[0], pair_recv.at[0], pair)
    got_grad = remote(grads.at[z, other_rows], grads.at[z, other_rows], pair_send.at[1], pair_recv.at[1], pair)
    pair_info.start()

    for n in range(1, AHEAD):
        multiply(n)
        send(n)

    @pl.loop(0, n_z)
    def _(b):
        grad_load(b).wait()

    got_info.wait_recv()
    pair_grad.start()
    per_q = rows_ref.shape[1]
    experts_here = n_q

    def chosen_mask():
        code = jnp.concatenate([info[0, 1], info[1, 1]], axis=1)
        spot = lax.broadcasted_iota(jnp.int32, (experts_here, per_q, 2 * toks), 1).astype(jnp.float32)
        return jnp.broadcast_to(code[:, None, :], spot.shape) == spot

    mask = chosen_mask()
    gate = jnp.concatenate([info[0, 0], info[1, 0]], axis=1)
    spread = jnp.where(mask, jnp.broadcast_to(gate[:, None, :], mask.shape), 0.0)
    spread = spread.reshape(experts_here * per_q, 2 * toks)
    chosen[...] = jnp.where(mask, 1.0, 0.0).reshape(spread.shape).astype(jnp.bfloat16)
    turned = spread.T
    high = turned.astype(jnp.bfloat16)
    mix[0] = high
    mix[1] = (turned - high.astype(jnp.float32)).astype(jnp.bfloat16)
    row_gate[...] = jnp.broadcast_to(jnp.sum(spread, axis=1, keepdims=True), row_gate.shape)
    dots[...] = jnp.zeros(dots.shape, jnp.float32)

    def rg_copy(k):
        to = lax.rem(q + k, n_q)
        return remote(grad_out.at[to], slot_grad_ref.at[q], rg_send.at[to], rg_recv.at[q], at_q(k))

    def rg_wait(k):
        come = lax.rem(q + k, n_q)
        return remote(grad_out.at[come], slot_grad_ref.at[come], rg_send.at[come], rg_recv.at[come], at_q(k))

    def mg_copy(b, device):
        here = grads.at[b, other_rows]
        return remote(here, here, mg_send.at[b], mg_recv.at[b], device)

    def mg_copy_low(b, device):
        here = grads.at[b, other_rows]
        return remote(here, here, mg_send.at[n_z + b], mg_recv.at[b], device)

    def mg_step(j):
        below, above = z - j, z + j

        @pl.when((j > 0) & (below >= 0))
        def _():
            mg_copy(below, lower).wait_recv()

        @pl.when((j > 0) & (above <= last))
        def _():
            mg_copy(above, upper).wait_recv()

        @pl.when((below >= 0) & (z < last))
        def _():
            mg_copy(below, upper).start()

        @pl.when((above <= last) & (z > 0))
        def _():
            mg_copy_low(above, lower).start()

    def mg_finish(j):
        below, above = z - j, z + j

        @pl.when((below >= 0) & (z < last))
        def _():
            mg_copy(below, upper).wait_send()

        @pl.when((above <= last) & (z > 0))
        def _():
            mg_copy_low(above, lower).wait_send()

    def mixed(b):
        rows = arrived[b].reshape(n_q * per_q, cols)
        return jnp.dot(mix[0], rows, preferred_element_type=jnp.float32) + jnp.dot(
            mix[1], rows, preferred_element_type=jnp.float32
        )

    def add_dots(b):
        rows = arrived[b].reshape(n_q * per_q, cols)
        dots[...] += lax.dot_general(
            rows, grads[b], (((1,), (1,)), ((), ())), preferred_element_type=jnp.float32
        )

    def far_dots(n):
        @pl.when(z + n <= last)
        def _():
            add_dots(z + n)

        @pl.when(z - n >= 0)
        def _():
            add_dots(z - n)

    def z_copy(b, slot, s, device):
        span = pl.ds(s * toks, toks)
        return remote(
            passed_out.at[b, span], passed_in.at[slot, span], z_send.at[b, s], z_recv.at[slot, s], device
        )

    def x_wait_all(b):
        @pl.loop(1, n_q)
        def _(k):
            x_wait(b, k).wait_recv()

    @pl.loop(0, last)
    def _(n):
        b = block_at(n)
        x_wait_all(b)

        total[...] = mixed(b)
        up = b > z
        fed = (up & (z > 0)) | (jnp.logical_not(up) & (z < last))
        for s in range(2):
            span = pl.ds(s * toks, toks)

            @pl.when(fed)
            def _():
                z_copy(b, b, s, lower).wait_recv()
                total[span, :] += passed_in[b, span].astype(jnp.float32)

            passed_out[b, span] = total[span, :].astype(jnp.bfloat16)

            @pl.when(up)
            def _():
                z_copy(b, b, s, upper).start()

            @pl.when(b < z - 1)
            def _():
                z_copy(b, b, s, lower).start()

            @pl.when(b == z - 1)
            def _():
                z_copy(b, n_z, s, lower).start()

        @pl.when(n + AHEAD < n_z)
        def _():
            multiply(n + AHEAD)
            send(n + AHEAD)

        @pl.when(n == 0)
        def _():
            got_grad.wait_recv()
            picked_grad = jnp.dot(chosen[...], grads[z], preferred_element_type=jnp.float32)
            grad_out[...] = (picked_grad * row_gate[:, :1]).astype(jnp.bfloat16).reshape(grad_out.shape)
            slot_grad_ref[q] = grad_out[q]

        mg_step(n)

        @pl.when(n == n_z // 2)
        def _():
            @pl.loop(0, n_z // 2)
            def _(m):
                early = block_at(m)

                @pl.when((early - z <= n_z // 2) & (z - early <= n_z // 2))
                def _():
                    add_dots(early)

        @pl.when(n >= n_z // 2)
        def _():
            add_dots(b)

        @pl.when(n > n_z // 2)
        def _():
            far_dots(n)

    mg_step(last)
    far_dots(last)
    x_wait_all(z)
    add_dots(z)
    gate_grad = jnp.where(chosen_mask(), dots[...].reshape(experts_here, per_q, 2 * toks), 0.0)
    gate_grad = jnp.sum(gate_grad, axis=1)
    gg_out[0] = gate_grad[:, :toks]
    gg_out[1] = gate_grad[:, toks:]
    gg_all[half * n_z + z] = gg_out[half]
    spot = half * n_z + z

    def gg_copy(k, slot):
        to = lax.rem(spot + k, 2 * n_z)
        to_half = to // n_z
        return remote(
            gg_out.at[to_half], gg_all.at[slot], gg_send.at[to], gg_recv.at[slot],
            (dp, to_half * n_q + q, lax.rem(to, n_z)),
        )

    @pl.loop(1, 2 * n_z)
    def _(k):
        gg_copy(k, spot).start()

    @pl.loop(1, n_q)
    def _(k):
        rg_copy(k).start()

    total[...] = mixed(z)

    for s in range(2):
        span = pl.ds(s * toks, toks)

        @pl.when(z > 0)
        def _():
            z_copy(z, z, s, lower).wait_recv()
            total[span, :] += passed_in[z, span].astype(jnp.float32)

        @pl.when(z < last)
        def _():
            z_copy(z, n_z, s, upper).wait_recv()
            total[span, :] += passed_in[n_z, span].astype(jnp.float32)

    comb_out[...] = total[other_rows, :].astype(jnp.bfloat16)
    pair_comb = remote(comb_out, comb_in, pair_send.at[2], pair_recv.at[2], pair)
    @pl.loop(1, 2 * n_z)
    def _(k):
        gg_copy(k, lax.rem(spot + k, 2 * n_z)).wait_recv()

    parts = []
    for h in range(2):
        summed = gg_all[h * n_z]
        for k in range(1, n_z):
            summed = summed + gg_all[h * n_z + k]
        parts.append(summed)
    gate_grad = jnp.concatenate(parts, axis=0)
    gate_values = gates[...]
    mix_term = jnp.sum(gate_values * gate_grad, axis=0, keepdims=True)
    logit_grad = gate_values * (gate_grad - mix_term)
    high = logit_grad.astype(jnp.bfloat16)
    rest = logit_grad - high.astype(jnp.float32)
    middle = rest.astype(jnp.bfloat16)
    low = (rest - middle.astype(jnp.float32)).astype(jnp.bfloat16)
    token_cols = token_all[:, pl.ds(pl.multiple_of(z * width, 128), width)]
    product = jnp.dot(low, token_cols, preferred_element_type=jnp.float32)
    product += jnp.dot(middle, token_cols, preferred_element_type=jnp.float32)
    product += jnp.dot(high, token_cols, preferred_element_type=jnp.float32)
    product = product * (1.0 / toks)
    each, lanes = experts // n_dp, width // 128
    for e in range(experts):
        for k in range(lanes):
            row = (e % each) * lanes + k
            part[e // each, row // 4, row % 4 : row % 4 + 1, :] = product[e : e + 1, k * 128 : (k + 1) * 128]

    def exchange(count, me, where, source, target, send, recv, meanwhile=None):
        def copy(k, slot):
            to = lax.rem(me + k, count)
            return remote(source(to), target(slot), send.at[to], recv.at[slot], where(k))

        @pl.loop(1, count)
        def _(k):
            copy(k, me).start()

        if meanwhile is not None:
            meanwhile()

        @pl.loop(1, count)
        def _(k):
            copy(k, lax.rem(me + k, count)).wait_recv()

        @pl.loop(1, count)
        def _(k):
            copy(k, me).wait_send()

    from_dp[dp] = part[dp]
    exchange(n_dp, dp, at_dp, lambda k: part.at[k], lambda k: from_dp.at[k], send1, recv1)
    summed = from_dp[0]
    for k in range(1, n_dp):
        summed = summed + from_dp[k]
    from_ctx[ctx] = summed
    exchange(n_ctx, ctx, at_ctx, lambda k: from_ctx.at[ctx], lambda k: from_ctx.at[k], send2, recv2)
    summed = from_ctx[0]
    for k in range(1, n_ctx):
        summed = summed + from_ctx[k]
    packed[...] = jnp.zeros(packed.shape, jnp.float32)
    for k in range(summed.shape[0]):
        packed[4 * k : 4 * k + 4, :] = summed[k]
    out_ref[dp, z] = packed[...].astype(jnp.bfloat16)
    exchange(n_z, z, at_z, lambda k: out_ref.at[dp, z], lambda k: out_ref.at[dp, k], send3, recv3, pair_comb.start)
    exchange(n_dp, dp, at_dp, lambda k: out_ref.at[dp], lambda k: out_ref.at[k], send4, recv4)

    remote(comb_out, comb_in, pair_send.at[2], pair_recv.at[2], pair).wait_recv()
    comb_ref[...] = (total[own_rows, :] + comb_in[...].astype(jnp.float32)).astype(jnp.bfloat16)

    @pl.loop(1, n_q)
    def _(k):
        rg_wait(k).wait_recv()

    pair_info.wait_send()
    pair_grad.wait_send()
    pair_comb.wait_send()

    @pl.loop(1, n_q)
    def _(k):
        rg_copy(k).wait_send()

    @pl.loop(1, 2 * n_z)
    def _(k):
        gg_copy(k, spot).wait_send()

    @pl.loop(0, n_z)
    def _(j):
        mg_finish(j)

        @pl.loop(1, n_q)
        def _(k):
            x_copy(j, k).wait_send()

        @pl.when(j != z)
        def _():
            z_copy(j, j, 0, lower).wait_send()
            z_copy(j, j, 1, lower).wait_send()


def layer(rows, weight, grad, ids, router_weight, tokens):
    n_dp, n_ctx, n_z = lax.axis_size("dp"), lax.axis_size("ctx"), lax.axis_size("tp")
    n_q = n_ctx // 2
    per_q, depth = rows.shape[1:]
    full = weight.shape[1]
    cols = full // n_z
    experts, toks = router_weight.shape[0], tokens.shape[0]
    width = tokens.shape[1] // n_z
    each, lanes = experts // n_dp, width // 128
    chunk = (each * lanes // 4, 4, 128)
    padded = -(-each * lanes // 16) * 16
    vmem = pl.BlockSpec(memory_space=pltpu.VMEM)
    anywhere = pl.BlockSpec(memory_space=pl.ANY)
    bf16, f32 = jnp.bfloat16, jnp.float32
    dma = pltpu.SemaphoreType.DMA
    scratch = [
        pltpu.VMEM((n_z, depth, cols), bf16),
        pltpu.VMEM((n_z, 2 * toks, cols), bf16),
        pltpu.VMEM(tokens.shape, bf16),
        pltpu.VMEM((n_z, n_q, per_q, cols), bf16),
        pltpu.VMEM((n_z, n_q, per_q, cols), bf16),
        pltpu.VMEM((n_z + 1, 2 * toks, cols), bf16),
        pltpu.VMEM((n_z, 2 * toks, cols), bf16),
        pltpu.VMEM((2, 2 * toks, n_q * per_q), bf16),
        pltpu.VMEM((n_q * per_q, 2 * toks), bf16),
        pltpu.VMEM((n_q * per_q, 2 * toks), f32),
        pltpu.VMEM((2 * toks, cols), f32),
        pltpu.VMEM((n_q * per_q, 128), f32),
        pltpu.VMEM((2, 2, n_q, toks), f32),
        pltpu.VMEM((2, 2, n_q, toks), f32),
        pltpu.VMEM((experts, toks), f32),
        pltpu.VMEM((2, n_q, toks), f32),
        pltpu.VMEM((2 * n_z, n_q, toks), f32),
        pltpu.VMEM((toks, cols), bf16),
        pltpu.VMEM((toks, cols), bf16),
        pltpu.VMEM((n_q, per_q, cols), bf16),
        pltpu.VMEM((n_dp,) + chunk, f32),
        pltpu.VMEM((n_dp,) + chunk, f32),
        pltpu.VMEM((n_ctx,) + chunk, f32),
        pltpu.VMEM((padded, 128), f32),
        dma((n_z,)), dma, dma((n_z,)),
        dma((n_z, n_q)), dma((n_z, n_q)),
        dma((n_z, 2)), dma((n_z + 1, 2)),
        dma((2 * n_z,)), dma((n_z,)),
        dma((3,)), dma((3,)),
        dma((n_q,)), dma((n_q,)),
        dma((2 * n_z,)), dma((2 * n_z,)),
        dma((n_dp,)), dma((n_dp,)), dma((n_ctx,)), dma((n_ctx,)),
        dma((n_z,)), dma((n_z,)), dma((n_dp,)), dma((n_dp,)),
    ]
    return pl.pallas_call(
        layer_kernel,
        out_shape=(
            jax.ShapeDtypeStruct((toks, cols), bf16),
            jax.ShapeDtypeStruct((n_q, per_q, cols), bf16),
            jax.ShapeDtypeStruct((n_dp, n_z, padded, 128), bf16),
        ),
        in_specs=[vmem, anywhere, anywhere, vmem, vmem, anywhere],
        out_specs=(vmem, vmem, vmem),
        scratch_shapes=scratch,
        compiler_params=pltpu.CompilerParams(collective_id=1, has_side_effects=True, vmem_limit_bytes=56 << 20),
        name="layer",
    )(rows, weight, grad, ids, router_weight, tokens)


def per_device(tokens, router_weight, expert_hidden, down_weight, expert_ids, mixed_grad):
    tp_ranks, dp_ranks = lax.axis_size("tp"), lax.axis_size("dp")
    hidden = expert_hidden[0, :, 0]
    capacity, sources, depth = hidden.shape
    experts = router_weight.shape[1]
    group = sources // 2
    rows = hidden.reshape(capacity, 2, group, depth).transpose(2, 1, 0, 3)
    rows = rows.reshape(group, 2 * capacity, depth)

    combined, slot_grads, router = layer(
        rows, down_weight[0], mixed_grad, expert_ids.T, router_weight.T, tokens
    )
    slot_grads = slot_grads.reshape(group, 2, capacity, slot_grads.shape[-1]).transpose(2, 1, 0, 3)
    row_grads = slot_grads.reshape(1, capacity, 1, sources, slot_grads.shape[-1])
    each = experts // dp_ranks
    lanes = tokens.shape[1] // tp_ranks // 128
    router = router[:, :, : each * lanes].astype(jnp.float32)
    router = router.reshape(dp_ranks, tp_ranks, each, lanes, 128).transpose(0, 2, 1, 3, 4)
    router_grad = router.reshape(experts, tokens.shape[1]).T
    return (combined, row_grads, router_grad)


def solution(mesh):
    return jax.shard_map(
        per_device,
        mesh=mesh,
        in_specs=(
            P(("dp", "ctx"), None),
            P(),
            P("dp", None, "ctx", None, "tp"),
            P("ctx", "tp", None),
            P(("dp", "ctx"), None),
            P(("dp", "ctx"), None),
        ),
        out_specs=(P(("dp", "ctx"), "tp"), P("dp", None, "ctx", None, "tp"), P()),
        check_vma=False,
    )
```
